128 devices in a mesh: layer: 2 (over x_lo), row: 8 (over x_hi, z), col: 8 (over y, core).
Axes of the slice: x: 4 (x_hi: 2, x_lo: 2; x = x_hi * 2 + x_lo), y: 4, z: 4, core: 2. Of those that a mesh axis runs over, the one named last changes fastest.
Arguments:
- grids: bfloat16 [4, 8192, 16384], P('layer', 'row', 'col'), may hold values from -6 to 6
- taper: float32 [8192], replicated, may hold values from 0.5 to 2
- w_steps: int32 [4], P('layer'), may hold values from -40 to 40
Outputs:
- image: float32 [8192, 8192], P(('layer', 'col'), 'row')
The draws below stay inside these ranges and needn't reach their ends.
All inputs are finite; a program needn't handle non-finite values.
Results may differ from the reference program's by a relative error of at most 0.01.
Values may be sent and summed in bfloat16 or wider, within the bound.
No kernel may reach another device: no remote copies, remote signals or barrier semaphores. Data moves between devices by JAX's collectives and lax.ppermute only.
A program may use at most 192 MiB of HBM per device.

```python
import math
import jax
import jax.numpy as jnp
from jax import lax

RADIX = 128
INNER = 64
NPIX = 8192
LAYERS = 4


def touch_ends(entries, stream_key, smallest, top_value):
    place = [jax.random.randint(jax.random.fold_in(stream_key, axis), (), 0, length) for axis, length in enumerate(entries.shape)]
    longest = entries.shape.index(max(entries.shape))
    neighbour = place[:longest] + [(place[longest] + 1) % entries.shape[longest]] + place[longest + 1:]
    return entries.at[tuple(place)].set(smallest).at[tuple(neighbour)].set(top_value)


def level_of(rng, extent, cuts, smallest, top_value):
    gain, own = 1.0, jax.random.fold_in(rng, 6)
    for position, blocks in cuts:
        steps = jnp.exp(jax.random.uniform(jax.random.fold_in(own, position), (blocks,), jnp.float32, smallest / len(cuts), top_value / len(cuts)))
        gain = gain * jnp.repeat(steps, extent[position] // blocks).reshape([-1 if axis == position else 1 for axis in range(len(extent))])
    return gain


def scatter_about(rng, dims, deviation, reach, split=(), kind=jnp.bfloat16):
    factor_of = level_of(rng, dims, split, -0.22, 0.18) if split else 1.0
    result = jax.random.normal(rng, dims, jnp.float32) * deviation * factor_of
    return jnp.minimum(jnp.maximum(result, -reach), reach).astype(kind)


def setup_inputs(seed: int = 0) -> dict:
    streams_of = jax.random.split(jax.random.key(seed), 4)
    grids = scatter_about(streams_of[0], (LAYERS, NPIX, 2 * NPIX), 1.0, 6.0, ((0, 2), (1, 8), (2, 8)))
    taper = jnp.clip(jnp.exp(jax.random.uniform(streams_of[1], (NPIX,), jnp.float32, math.log(0.5), math.log(2.0))), 0.5, 2.0)
    w_steps = touch_ends(jax.random.randint(streams_of[2], (LAYERS,), -40, 41), jax.random.fold_in(streams_of[2], 1), -40, 40).astype(jnp.int32)
    return {"grids": grids, "taper": taper, "w_steps": w_steps}


W_STEP = 1.0
TWO_PI = 2.0 * math.pi

def circle(product, count):
    angle = TWO_PI / count * (product % count).astype(jnp.float32)
    return (jnp.cos(angle), jnp.sin(angle))

def tables(count):
    steps = jnp.arange(count, dtype=jnp.int32)
    cosine, sine = circle(steps[:, None] * steps[None, :], count)
    cosine = lax.optimization_barrier(cosine.astype(jnp.bfloat16))
    sine = lax.optimization_barrier(sine.astype(jnp.bfloat16))
    return (cosine.astype(jnp.float32), sine.astype(jnp.float32))

def section(real, imag, cosine, sine, form):
    out_real = jnp.einsum(form, real, cosine) - jnp.einsum(form, imag, sine)
    out_imag = jnp.einsum(form, real, sine) + jnp.einsum(form, imag, cosine)
    return (out_real, out_imag)

def one_layer(grid_layer, w_value):
    cos_a, sin_a = tables(RADIX)
    cos_b, sin_b = tables(INNER)
    steps_a = jnp.arange(RADIX, dtype=jnp.int32)
    steps_b = jnp.arange(INNER, dtype=jnp.int32)
    tw_cos, tw_sin = circle(steps_a[:, None] * steps_b[None, :], NPIX)
    cells = grid_layer.astype(jnp.float32).reshape(NPIX, RADIX, 2, INNER)
    y_real, y_imag = section(cells[:, :, 0], cells[:, :, 1], cos_a, sin_a, 'uab,ac->ucb')
    z_real = (y_real * tw_cos - y_imag * tw_sin).astype(jnp.bfloat16).astype(jnp.float32)
    z_imag = (y_real * tw_sin + y_imag * tw_cos).astype(jnp.bfloat16).astype(jnp.float32)
    h_real, h_imag = section(z_real, z_imag, cos_b, sin_b, 'ucb,bd->udc')
    h_real = h_real.reshape(NPIX, NPIX).astype(jnp.bfloat16).astype(jnp.float32)
    h_imag = h_imag.reshape(NPIX, NPIX).astype(jnp.bfloat16).astype(jnp.float32)
    h_real = h_real.reshape(RADIX, INNER, NPIX)
    h_imag = h_imag.reshape(RADIX, INNER, NPIX)
    y_real, y_imag = section(h_real, h_imag, cos_a, sin_a, 'abm,ac->cbm')
    z_real = (y_real * tw_cos[:, :, None] - y_imag * tw_sin[:, :, None]).astype(jnp.bfloat16).astype(jnp.float32)
    z_imag = (y_real * tw_sin[:, :, None] + y_imag * tw_cos[:, :, None]).astype(jnp.bfloat16).astype(jnp.float32)
    f_real, f_imag = section(z_real, z_imag, cos_b, sin_b, 'cbm,bd->dcm')
    f_real = f_real.reshape(NPIX, NPIX)
    f_imag = f_imag.reshape(NPIX, NPIX)
    coords = (jnp.arange(NPIX, dtype=jnp.int32).astype(jnp.float32) - NPIX / 2) / NPIX
    height = jnp.sqrt(1.0 - coords[:, None] * coords[:, None] - coords[None, :] * coords[None, :])
    phase = TWO_PI * w_value * (height - 1.0)
    return jnp.cos(phase) * f_real - jnp.sin(phase) * f_imag

def reference(grids, taper, w_steps):
    w_values = w_steps.astype(jnp.float32) * W_STEP

    def accumulate(index, total):
        return total + one_layer(grids[index], w_values[index])
    summed = lax.fori_loop(0, LAYERS, accumulate, jnp.zeros((NPIX, NPIX), jnp.float32))
    return summed * (taper[:, None] * taper[None, :]) / NPIX
```

```python
import functools
import math

import jax
import jax.numpy as jnp
import numpy as np
from jax import lax
from jax.experimental import pallas as pl
from jax.experimental.pallas import tpu as pltpu
from jax.sharding import PartitionSpec as P

INNER = 64
NPIX = 8192
LANES = 128
GROUP = 8
LAYERS_AXIS = 2
BLOCK = NPIX // GROUP
ROWS = BLOCK // GROUP
CELLS = NPIX // ROWS
HALF_ROOT = math.sqrt(0.5)
VMEM_LIMIT = 60 * 1024 * 1024

SIN_TERMS = tuple((-1.0) ** n * math.pi ** (2 * n + 1) / math.factorial(2 * n + 1) for n in range(7))
COS_TERMS = tuple((-1.0) ** n * math.pi ** (2 * n) / math.factorial(2 * n) for n in range(7))


def unit(product, count):
    angle = 2.0 * np.pi / count * (product % count).astype(np.float64)
    return np.cos(angle), np.sin(angle)


def spread_tables():
    cell = np.arange(BLOCK).reshape(BLOCK // INNER, 1, INNER)
    cell = np.broadcast_to(cell, (BLOCK // INNER, 2, INNER)).reshape(1, 2 * BLOCK)
    cosine, sine = unit(np.arange(GROUP)[:, None] * cell, NPIX)
    return cosine.astype(np.float32), sine.astype(np.float32)


def wide_table():
    cell = np.arange(BLOCK).reshape(BLOCK // INNER, INNER, 1, 1)
    freq = np.arange(BLOCK).reshape(1, 1, GROUP, LANES)
    cosine, sine = unit(cell * freq, BLOCK)
    upper = np.stack([cosine, sine], axis=3)
    lower = np.stack([-sine, cosine], axis=3)
    return np.stack([upper, lower], axis=1).reshape(2 * BLOCK, 2 * BLOCK).astype(jnp.bfloat16)


def short_table():
    steps = np.arange(ROWS)
    cosine, sine = unit(steps[:, None] * steps[None, :], ROWS)
    upper = np.concatenate([cosine, -sine], axis=1)
    lower = np.concatenate([sine, cosine], axis=1)
    return np.concatenate([upper, lower], axis=0).astype(jnp.bfloat16)


def row_tables():
    cosine, sine = unit(np.arange(ROWS)[:, None] * np.arange(CELLS)[None, :], NPIX)
    return cosine.astype(np.float32), sine.astype(np.float32)


def along_v_kernel(cells_ref, cos_ref, sin_ref, table_ref, out_ref, spun):
    @pl.when(pl.program_id(0) == 0)
    def _():
        lane = lax.broadcasted_iota(jnp.int32, (16, LANES), 1)
        sign = jnp.where(lane < INNER, -1.0, 1.0)

        def turn(z):
            return pltpu.roll(z, INNER, 1) * sign

        def one_tile(tile, carry):
            rows = pl.ds(pl.multiple_of(tile * 16, 16), 16)
            for a in range(2 * BLOCK // LANES):
                lanes = pl.ds(a * LANES, LANES)
                x = [cells_ref[c, rows, lanes].astype(jnp.float32) for c in range(GROUP)]
                e = [x[c] + x[c + 4] for c in range(4)]
                d = [x[c] - x[c + 4] for c in range(4)]
                even, odd = e[0] + e[2], e[1] + e[3]
                near, far = (d[1] - d[3]) * HALF_ROOT, (d[1] + d[3]) * HALF_ROOT

                def put(j, z):
                    spun[j, rows, lanes] = z.astype(jnp.bfloat16)

                put(0, even + odd)
                z = even - odd
                put(4, z * cos_ref[4:5, lanes] + turn(z) * sin_ref[4:5, lanes])
                for j, p, q in ((2, e[0] - e[2], e[1] - e[3]), (1, d[0] + near, d[2] + far), (3, d[0] - near, far - d[2])):
                    jp, jq = turn(p), turn(q)
                    put(j, (p + jq) * cos_ref[j : j + 1, lanes] + (jp - q) * sin_ref[j : j + 1, lanes])
                    o = GROUP - j
                    put(o, (p - jq) * cos_ref[o : o + 1, lanes] + (jp + q) * sin_ref[o : o + 1, lanes])
            return carry

        lax.fori_loop(0, ROWS // 16, one_tile, 0)

    for j in range(GROUP):
        res = jnp.dot(spun[j], table_ref[...], preferred_element_type=jnp.float32)
        out_ref[0, j, 0] = res[:, :LANES].astype(jnp.bfloat16)
        out_ref[0, j, 1] = res[:, LANES:].astype(jnp.bfloat16)


def along_v(cells):
    tw_cos, tw_sin = spread_tables()
    whole = lambda *shape: pl.BlockSpec(shape, lambda s: (0,) * len(shape))
    return pl.pallas_call(
        along_v_kernel,
        grid=(GROUP,),
        out_shape=jax.ShapeDtypeStruct((GROUP, GROUP, 2, ROWS, LANES), jnp.bfloat16),
        in_specs=[
            whole(GROUP, ROWS, 2 * BLOCK),
            whole(GROUP, 2 * BLOCK),
            whole(GROUP, 2 * BLOCK),
            pl.BlockSpec((2 * BLOCK, 2 * LANES), lambda s: (0, s)),
        ],
        out_specs=pl.BlockSpec((1, GROUP, 2, ROWS, LANES), lambda s: (s, 0, 0, 0, 0)),
        scratch_shapes=[pltpu.VMEM((GROUP, ROWS, 2 * BLOCK), jnp.bfloat16)],
        compiler_params=pltpu.CompilerParams(vmem_limit_bytes=VMEM_LIMIT),
        cost_estimate=pl.CostEstimate(flops=2 * 1024 * 2048 * 2048, bytes_accessed=16 << 20, transcendentals=0),
        name="along_v",
    )(cells, jnp.asarray(tw_cos), jnp.asarray(tw_sin), jnp.asarray(wide_table()))


def eight(xr, xi):
    er = [xr[c] + xr[c + 4] for c in range(4)]
    ei = [xi[c] + xi[c + 4] for c in range(4)]
    dr = [xr[c] - xr[c + 4] for c in range(4)]
    di = [xi[c] - xi[c + 4] for c in range(4)]
    evr, evi, odr, odi = er[0] + er[2], ei[0] + ei[2], er[1] + er[3], ei[1] + ei[3]
    nr, ni = (dr[1] - dr[3]) * HALF_ROOT, (di[1] - di[3]) * HALF_ROOT
    fr, fi = (dr[1] + dr[3]) * HALF_ROOT, (di[1] + di[3]) * HALF_ROOT
    outr, outi = [None] * 8, [None] * 8
    outr[0], outi[0] = evr + odr, evi + odi
    outr[4], outi[4] = evr - odr, evi - odi
    pairs = (
        (2, er[0] - er[2], ei[0] - ei[2], er[1] - er[3], ei[1] - ei[3]),
        (1, dr[0] + nr, di[0] + ni, dr[2] + fr, di[2] + fi),
        (3, dr[0] - nr, di[0] - ni, fr - dr[2], fi - di[2]),
    )
    for j, pr, pi, qr, qi in pairs:
        outr[j], outi[j] = pr - qi, pi + qr
        outr[8 - j], outi[8 - j] = pr + qi, pi - qr
    return outr, outi


def along_u_kernel(first, last, place_ref, w_ref, cells_ref, cos_ref, sin_ref, table_ref, *rest):
    if first:
        out_ref, mid, spun = rest
    else:
        sofar_ref, out_ref, mid, spun = rest
    step = pl.program_id(0)
    tiles = ROWS // 16

    @pl.when(step < tiles)
    def _():
        for c in range(GROUP):
            xr = [cells_ref[GROUP * r + c, 0].astype(jnp.float32) for r in range(GROUP)]
            xi = [cells_ref[GROUP * r + c, 1].astype(jnp.float32) for r in range(GROUP)]
            yr, yi = eight(xr, xi)
            for i in range(GROUP):
                wr, wi = math.cos(2 * math.pi * c * i / CELLS), math.sin(2 * math.pi * c * i / CELLS)
                if c * i == 0:
                    mid[i, c, 0], mid[i, c, 1] = yr[i], yi[i]
                else:
                    mid[i, c, 0] = yr[i] * wr - yi[i] * wi
                    mid[i, c, 1] = yr[i] * wi + yi[i] * wr
        rows = pl.ds(pl.multiple_of(step * 16, 16), 16)
        lower = pl.ds(pl.multiple_of(ROWS + step * 16, 16), 16)
        for i1 in range(GROUP):
            yr, yi = eight([mid[i1, c, 0] for c in range(GROUP)], [mid[i1, c, 1] for c in range(GROUP)])
            for i2 in range(GROUP):
                i = i1 + GROUP * i2
                tc, ts = cos_ref[:, i : i + 1], sin_ref[:, i : i + 1]
                lanes = slice(i * LANES, (i + 1) * LANES)
                spun[rows, lanes] = (yr[i2] * tc - yi[i2] * ts).astype(jnp.bfloat16)
                spun[lower, lanes] = (yr[i2] * ts + yi[i2] * tc).astype(jnp.bfloat16)

    @pl.when(step >= tiles)
    def _():
        block = step - tiles
        lanes = pl.ds(pl.multiple_of(block * GROUP * LANES, LANES), GROUP * LANES)
        full = jnp.dot(table_ref[...], spun[:, lanes], preferred_element_type=jnp.float32)
        shape = (ROWS, LANES)
        g = lax.broadcasted_iota(jnp.int32, shape, 0)
        q = lax.broadcasted_iota(jnp.int32, shape, 1)
        m = place_ref[0] + GROUP * q
        down = (m.astype(jnp.float32) - NPIX / 2) / NPIX
        rest_down = 1.0 - down * down
        w_value = w_ref[0].astype(jnp.float32)
        images = []
        for n in range(GROUP):
            l = CELLS * g + (block * GROUP + n)
            across = (l.astype(jnp.float32) - NPIX / 2) / NPIX
            turns = w_value * (jnp.sqrt(rest_down - across * across) - 1.0)
            t = turns - jnp.floor(turns + 0.5)
            t2 = t * t
            sine, cosine = SIN_TERMS[-1], COS_TERMS[-1]
            for a, b in zip(SIN_TERMS[-2::-1], COS_TERMS[-2::-1]):
                sine, cosine = sine * t2 + a, cosine * t2 + b
            sine = sine * t
            real = full[:ROWS, n * LANES : (n + 1) * LANES]
            imag = full[ROWS:, n * LANES : (n + 1) * LANES]
            image = real - 2.0 * sine * (sine * real + cosine * imag)
            if not first:
                image = image + sofar_ref[:, n * LANES : (n + 1) * LANES]
            images.append(image)
        if not last:
            for n in range(GROUP):
                out_ref[:, n * LANES : (n + 1) * LANES] = images[n]
        else:
            for n in range(0, GROUP, 2):
                pair = [z.reshape(ROWS // 8, 8, LANES) for z in images[n : n + 2]]
                both = jnp.concatenate(pair, axis=1).astype(jnp.bfloat16)
                out_ref[:, 8 * n : 8 * n + 16, :] = both


def along_u(cells, place, w_value, sofar, last):
    first = sofar is None
    tiles = ROWS // 16
    tw_cos, tw_sin = row_tables()
    late = lambda s: jnp.maximum(s - tiles, 0)
    early = lambda s: jnp.minimum(s, tiles - 1)
    smem = pl.BlockSpec(memory_space=pltpu.SMEM)
    in_specs = [
        smem,
        smem,
        pl.BlockSpec((CELLS, 2, 16, LANES), lambda s: (0, 0, early(s), 0)),
        pl.BlockSpec((16, CELLS), lambda s: (early(s), 0)),
        pl.BlockSpec((16, CELLS), lambda s: (early(s), 0)),
        pl.BlockSpec((2 * ROWS, 2 * ROWS), lambda s: (0, 0)),
    ]
    args = [place, w_value, cells, jnp.asarray(tw_cos), jnp.asarray(tw_sin), jnp.asarray(short_table())]
    if not first:
        in_specs.append(pl.BlockSpec((ROWS, GROUP * LANES), lambda s: (0, late(s))))
        args.append(sofar)
    if last:
        out_shape = jax.ShapeDtypeStruct((ROWS // 8, 8 * CELLS, LANES), jnp.bfloat16)
        out_spec = pl.BlockSpec((ROWS // 8, 8 * GROUP, LANES), lambda s: (0, late(s), 0))
    else:
        out_shape = jax.ShapeDtypeStruct((ROWS, CELLS * LANES), jnp.float32)
        out_spec = pl.BlockSpec((ROWS, GROUP * LANES), lambda s: (0, late(s)))
    return pl.pallas_call(
        functools.partial(along_u_kernel, first, last),
        grid=(tiles + CELLS // GROUP,),
        out_shape=out_shape,
        in_specs=in_specs,
        out_specs=out_spec,
        scratch_shapes=[
            pltpu.VMEM((GROUP, GROUP, 2, 16, LANES), jnp.float32),
            pltpu.VMEM((2 * ROWS, CELLS * LANES), jnp.bfloat16),
        ],
        compiler_params=pltpu.CompilerParams(vmem_limit_bytes=VMEM_LIMIT),
        cost_estimate=pl.CostEstimate(flops=2 * 256 * 256 * 8192, bytes_accessed=8 << 20, transcendentals=0),
        name="along_u",
    )(*args)


def arrange_kernel(cells_ref, rows_ref, cols_ref, out_ref):
    count = 8 * CELLS
    total = None
    q = lax.broadcasted_iota(jnp.int32, (LANES, BLOCK), 0)
    m = lax.broadcasted_iota(jnp.int32, (LANES, BLOCK), 1)
    for j in range(GROUP):
        pick = jnp.where(m == GROUP * q + j, 1.0, 0.0).astype(jnp.bfloat16)
        part = jnp.dot(cells_ref[j], pick, preferred_element_type=jnp.float32)
        total = part if total is None else total + part
    l = lax.broadcasted_iota(jnp.int32, (count, count), 0)
    held = lax.broadcasted_iota(jnp.int32, (count, count), 1)
    pick = jnp.where(held == 8 * (l % CELLS) + l // CELLS, 1.0, 0.0).astype(jnp.bfloat16)
    total = jnp.dot(pick, total.astype(jnp.bfloat16), preferred_element_type=jnp.float32)
    out_ref[...] = total * (rows_ref[...] * cols_ref[...]) / NPIX


def arrange(cells, taper_rows, taper_cols):
    vmem = pl.BlockSpec(memory_space=pltpu.VMEM)
    return pl.pallas_call(
        arrange_kernel,
        out_shape=jax.ShapeDtypeStruct((8 * CELLS, BLOCK), jnp.float32),
        in_specs=[vmem] * 3,
        out_specs=vmem,
        compiler_params=pltpu.CompilerParams(vmem_limit_bytes=VMEM_LIMIT),
        name="arrange",
    )(cells, taper_rows, taper_cols)


def on_device(grids, taper, w_steps):
    lay, row, col = lax.axis_index("layer"), lax.axis_index("row"), lax.axis_index("col")
    local = grids.shape[0]
    place = (BLOCK * row + col).astype(jnp.int32).reshape(1)
    taper_cols = lax.dynamic_slice_in_dim(taper, BLOCK * row, BLOCK).reshape(1, BLOCK)
    taper_rows = lax.dynamic_slice_in_dim(taper, 8 * CELLS * (GROUP * lay + col), 8 * CELLS).reshape(8 * CELLS, 1)
    image = None
    for k in range(local):
        cells = lax.all_to_all(
            grids[k].reshape(GROUP, ROWS, 2 * BLOCK), "col", split_axis=0, concat_axis=0, tiled=True
        )
        half = along_v(cells).reshape(GROUP * GROUP, 2, ROWS, LANES)
        half = lax.all_to_all(half, ("row", "col"), split_axis=0, concat_axis=0, tiled=True)
        image = along_u(half, place, w_steps[k : k + 1], image, k == local - 1)
    image = image.reshape(LAYERS_AXIS, GROUP, 8 * CELLS, LANES)
    keep = lax.dynamic_index_in_dim(image, lay, 0, keepdims=False)
    send = lax.dynamic_index_in_dim(image, 1 - lay, 0, keepdims=False)
    other = lax.ppermute(send, "layer", [(0, 1), (1, 0)])
    summed = (keep.astype(jnp.float32) + other.astype(jnp.float32)).astype(jnp.bfloat16)
    tiles = lax.all_to_all(summed, "col", split_axis=0, concat_axis=0, tiled=True)
    return arrange(tiles, taper_rows, taper_cols)


def solution(mesh):
    placed = (P("layer", "row", "col"), P(), P("layer"))
    return jax.shard_map(
        on_device, mesh=mesh, in_specs=placed, out_specs=P(("layer", "col"), "row"), check_vma=False
    )
```

```python
import functools
import math

import jax
import jax.numpy as jnp
import numpy as np
from jax import lax
from jax.experimental import pallas as pl
from jax.experimental.pallas import tpu as pltpu
from jax.sharding import PartitionSpec as P

INNER = 64
NPIX = 8192
LANES = 128
GROUP = 8
LAYERS_AXIS = 2
BLOCK = NPIX // GROUP
ROWS = BLOCK // GROUP
CELLS = NPIX // ROWS
HALF_ROOT = math.sqrt(0.5)
VMEM_LIMIT = 60 * 1024 * 1024


def power_terms(f):
    line = np.polynomial.Chebyshev.interpolate(lambda z: f(np.sqrt(z)), 4, domain=[0.0, 0.25])
    return [float(c) for c in line.convert(kind=np.polynomial.Polynomial).coef]


SIN_TERMS = power_terms(lambda t: np.pi * np.sinc(t))
COS_TERMS = power_terms(lambda t: np.cos(np.pi * t))


def unit(product, count):
    angle = 2.0 * np.pi / count * (product % count).astype(np.float64)
    return np.cos(angle), np.sin(angle)


def spread_tables():
    cell = np.arange(BLOCK) + BLOCK * np.arange(GROUP).reshape(GROUP, 1, 1)
    cosine, sine = unit(np.arange(GROUP)[:, None] * cell, NPIX)
    return cosine.astype(np.float32), sine.astype(np.float32)


def wide_table():
    cell = np.arange(BLOCK).reshape(GROUP, LANES, 1, 1)
    freq = np.arange(BLOCK).reshape(1, 1, GROUP, LANES)
    cosine, sine = unit(cell * freq, BLOCK)
    upper = np.stack([cosine, sine], axis=3)
    lower = np.stack([-sine, cosine], axis=3)
    return np.stack([upper, lower], axis=1).reshape(2 * BLOCK, 2 * BLOCK).astype(jnp.bfloat16)


def short_table():
    steps = np.arange(ROWS)
    cosine, sine = unit(steps[:, None] * steps[None, :], ROWS)
    upper = np.concatenate([cosine, -sine], axis=1)
    lower = np.concatenate([sine, cosine], axis=1)
    return np.concatenate([upper, lower], axis=0).astype(jnp.bfloat16)


def row_tables():
    start = np.arange(ROWS) + BLOCK * np.arange(GROUP)[:, None]
    cosine, sine = unit(start[:, :, None] * np.arange(CELLS), NPIX)
    return cosine.astype(np.float32), sine.astype(np.float32)


def eight(xr, xi):
    er = [xr[c] + xr[c + 4] for c in range(4)]
    ei = [xi[c] + xi[c + 4] for c in range(4)]
    dr = [xr[c] - xr[c + 4] for c in range(4)]
    di = [xi[c] - xi[c + 4] for c in range(4)]
    evr, evi, odr, odi = er[0] + er[2], ei[0] + ei[2], er[1] + er[3], ei[1] + ei[3]
    nr, ni = (dr[1] - dr[3]) * HALF_ROOT, (di[1] - di[3]) * HALF_ROOT
    fr, fi = (dr[1] + dr[3]) * HALF_ROOT, (di[1] + di[3]) * HALF_ROOT
    outr, outi = [None] * 8, [None] * 8
    outr[0], outi[0] = evr + odr, evi + odi
    outr[4], outi[4] = evr - odr, evi - odi
    pairs = (
        (2, er[0] - er[2], ei[0] - ei[2], er[1] - er[3], ei[1] - ei[3]),
        (1, dr[0] + nr, di[0] + ni, dr[2] + fr, di[2] + fi),
        (3, dr[0] - nr, di[0] - ni, fr - dr[2], fi - di[2]),
    )
    for j, pr, pi, qr, qi in pairs:
        outr[j], outi[j] = pr - qi, pi + qr
        outr[8 - j], outi[8 - j] = pr + qi, pi - qr
    return outr, outi


def part_planes(pair):
    one, two = pair[:, :LANES].astype(jnp.float32), pair[:, LANES:].astype(jnp.float32)
    low = lax.broadcasted_iota(jnp.int32, one.shape, 1) < INNER
    real = jnp.where(low, one, pltpu.roll(two, INNER, 1))
    imag = jnp.where(low, pltpu.roll(one, INNER, 1), two)
    return real, imag


def screened(real, imag, l, m, w_value):
    across = (l.astype(jnp.float32) - NPIX / 2) / NPIX
    down = (m.astype(jnp.float32) - NPIX / 2) / NPIX
    square = 1.0 - across * across - down * down
    turns = w_value * (square * lax.rsqrt(square) - 1.0)
    t = turns - jnp.floor(turns + 0.5)
    t2 = t * t
    sine, cosine = SIN_TERMS[-1], COS_TERMS[-1]
    for a, b in zip(SIN_TERMS[-2::-1], COS_TERMS[-2::-1]):
        sine, cosine = sine * t2 + a, cosine * t2 + b
    sine = sine * t
    return real - 2.0 * sine * (sine * real + cosine * imag)


def along_v_kernel(early, core_ref, place_ref, w_ref, _, *refs):
    cells, (cos_ref, sin_ref, table_ref, out_ref, spun) = refs[:-5], refs[-5:]
    step = pl.program_id(0)

    @pl.when(step == 0)
    def _():
        def one_tile(tile, carry):
            rows = pl.ds(pl.multiple_of(tile * 16, 16), 16)
            for part in range(GROUP):
                if early:
                    lanes = slice(2 * LANES * part, 2 * LANES * (part + 1))
                    pairs = [part_planes(ref[0, rows, lanes]) for ref in cells]
                    xr, xi = [p[0] for p in pairs], [p[1] for p in pairs]
                else:
                    xr = [cells[0][part, c, 0, rows].astype(jnp.float32) for c in range(GROUP)]
                    xi = [cells[0][part, c, 1, rows].astype(jnp.float32) for c in range(GROUP)]
                yr, yi = eight(xr, xi)
                lanes = slice(part * LANES, (part + 1) * LANES)
                for j in range(GROUP):
                    real, imag = yr[j], yi[j]
                    if j:
                        tc, ts = cos_ref[j : j + 1, lanes], sin_ref[j : j + 1, lanes]
                        real, imag = real * tc - imag * ts, real * ts + imag * tc
                    spun[j, rows, 2 * LANES * part : 2 * LANES * part + LANES] = real.astype(jnp.bfloat16)
                    spun[j, rows, 2 * LANES * part + LANES : 2 * LANES * (part + 1)] = imag.astype(jnp.bfloat16)
            return carry

        lax.fori_loop(0, ROWS // 16, one_tile, 0)

    shape = (ROWS, LANES)
    row = lax.broadcasted_iota(jnp.int32, shape, 0)
    q = lax.broadcasted_iota(jnp.int32, shape, 1)
    for j in range(GROUP):
        res = jnp.dot(spun[j], table_ref[...], preferred_element_type=jnp.float32)
        real, imag = res[:, :LANES], res[:, LANES:]
        if early:
            out_ref[0, j, 0] = real.astype(jnp.bfloat16)
            out_ref[0, j, 1] = imag.astype(jnp.bfloat16)
        else:
            l = row // CELLS * (NPIX // 2) + row % 8 * CELLS + row // 8 % 8 + place_ref[0]
            m = step * BLOCK + GROUP * q + j
            image = screened(real, imag, l, m, w_ref[0].astype(jnp.float32)).astype(jnp.bfloat16)
            out_ref[0, 0, j] = image[:CELLS]
            out_ref[1, 0, j] = image[CELLS:]


def along_v(early, cells, tw_cos, tw_sin, core, place, w_value, after):
    whole = lambda *shape: pl.BlockSpec(shape, lambda s, core: (0,) * len(shape))
    smem = pl.BlockSpec(memory_space=pltpu.SMEM)
    if early:
        shape, block, index = (GROUP, GROUP, 2, ROWS, LANES), (1, GROUP, 2, ROWS, LANES), lambda s, core: (s, 0, 0, 0, 0)
        pick = lambda k: pl.BlockSpec((1, ROWS, 2 * BLOCK), lambda s, core: (lax.rem(core[0] + k, 2), 0, 0))
        in_specs = [pick(k) for _ in range(GROUP // 2) for k in range(2)]
        cells = [pair for pair in cells for _ in range(2)]
    else:
        shape, block = (LAYERS_AXIS, GROUP, GROUP, CELLS, LANES), (LAYERS_AXIS, 1, GROUP, CELLS, LANES)
        index = lambda s, core: (0, s, 0, 0, 0)
        in_specs = [whole(GROUP, GROUP, 2, ROWS, LANES)]
    return pl.pallas_call(
        functools.partial(along_v_kernel, early),
        out_shape=jax.ShapeDtypeStruct(shape, jnp.bfloat16),
        grid_spec=pltpu.PrefetchScalarGridSpec(
            num_scalar_prefetch=1,
            grid=(GROUP,),
            in_specs=[
                smem,
                smem,
                pl.BlockSpec(memory_space=pl.ANY),
                *in_specs,
                whole(GROUP, BLOCK),
                whole(GROUP, BLOCK),
                pl.BlockSpec((2 * BLOCK, 2 * LANES), lambda s, core: (0, s)),
            ],
            out_specs=pl.BlockSpec(block, index),
            scratch_shapes=[pltpu.VMEM((GROUP, ROWS, 2 * BLOCK), jnp.bfloat16)],
        ),
        compiler_params=pltpu.CompilerParams(vmem_limit_bytes=VMEM_LIMIT),
        cost_estimate=pl.CostEstimate(flops=2 * 1024 * 2048 * 2048, bytes_accessed=16 << 20, transcendentals=0),
        name="v_first" if early else "v_last",
    )(core, place, w_value, after, *cells, tw_cos, tw_sin, jnp.asarray(wide_table()))


def along_u_kernel(early, place_ref, w_ref, _, *refs):
    cells, (cos_ref, sin_ref, table_ref, out_ref, mid, spun) = refs[:-6], refs[-6:]
    step = pl.program_id(0)
    tiles = ROWS // 16

    @pl.when(step < tiles)
    def _():
        for c in range(GROUP):
            if early:
                pairs = [part_planes(cells[r][c]) for r in range(GROUP)]
                xr, xi = [p[0] for p in pairs], [p[1] for p in pairs]
            else:
                xr = [cells[0][GROUP * r + c, 0].astype(jnp.float32) for r in range(GROUP)]
                xi = [cells[0][GROUP * r + c, 1].astype(jnp.float32) for r in range(GROUP)]
            yr, yi = eight(xr, xi)
            for i in range(GROUP):
                wr, wi = math.cos(2 * math.pi * c * i / CELLS), math.sin(2 * math.pi * c * i / CELLS)
                if c * i == 0:
                    mid[i, c, 0], mid[i, c, 1] = yr[i], yi[i]
                else:
                    mid[i, c, 0] = yr[i] * wr - yi[i] * wi
                    mid[i, c, 1] = yr[i] * wi + yi[i] * wr
        rows = pl.ds(pl.multiple_of(step * 16, 16), 16)
        lower = pl.ds(pl.multiple_of(ROWS + step * 16, 16), 16)
        for i1 in range(GROUP):
            yr, yi = eight([mid[i1, c, 0] for c in range(GROUP)], [mid[i1, c, 1] for c in range(GROUP)])
            for i2 in range(GROUP):
                i = i1 + GROUP * i2
                tc, ts = cos_ref[:, i : i + 1], sin_ref[:, i : i + 1]
                lanes = slice(i * LANES, (i + 1) * LANES)
                spun[rows, lanes] = (yr[i2] * tc - yi[i2] * ts).astype(jnp.bfloat16)
                spun[lower, lanes] = (yr[i2] * ts + yi[i2] * tc).astype(jnp.bfloat16)

    @pl.when(step >= tiles)
    def _():
        block = step - tiles
        lanes = pl.ds(pl.multiple_of(block * GROUP * LANES, LANES), GROUP * LANES)
        full = jnp.dot(table_ref[...], spun[:, lanes], preferred_element_type=jnp.float32)
        shape = (ROWS, LANES)
        g = lax.broadcasted_iota(jnp.int32, shape, 0)
        m = place_ref[0] + GROUP * lax.broadcasted_iota(jnp.int32, shape, 1)

        def by_tile(first, second):
            both = [z.reshape(ROWS // 8, 8, LANES) for z in (first, second)]
            return jnp.concatenate(both, axis=1).astype(jnp.bfloat16)

        for n in range(0, GROUP, 2):
            real = [full[:ROWS, k * LANES : (k + 1) * LANES] for k in (n, n + 1)]
            imag = [full[ROWS:, k * LANES : (k + 1) * LANES] for k in (n, n + 1)]
            if early:
                for p, pair in enumerate((real, imag)):
                    both = by_tile(*pair)
                    for group in range(LAYERS_AXIS):
                        out_ref[0, :, p, group, 8 * n : 8 * n + 16, :] = both[GROUP * group : GROUP * (group + 1)]
            else:
                images = [
                    screened(real[k], imag[k], CELLS * g + (block * GROUP + n + k), m, w_ref[0].astype(jnp.float32))
                    for k in range(2)
                ]
                out_ref[:, 8 * n : 8 * n + 16, :] = by_tile(*images)


def along_u(early, cells, tw_cos, tw_sin, place, w_value, after):
    tiles = ROWS // 16
    late = lambda s: jnp.maximum(s - tiles, 0)
    soon = lambda s: jnp.minimum(s, tiles - 1)
    smem = pl.BlockSpec(memory_space=pltpu.SMEM)
    if early:
        in_specs = [pl.BlockSpec((GROUP, 16, 2 * LANES), lambda s: (0, soon(s), 0))] * GROUP
        shape = (GROUP, GROUP, 2, LAYERS_AXIS, CELLS, LANES)
        out_spec = pl.BlockSpec((1,) + shape[1:], lambda s: (late(s), 0, 0, 0, 0, 0))
    else:
        in_specs = [pl.BlockSpec((CELLS, 2, 16, LANES), lambda s: (0, 0, soon(s), 0))]
        shape = (ROWS // 8, 8 * CELLS, LANES)
        out_spec = pl.BlockSpec((ROWS // 8, 8 * GROUP, LANES), lambda s: (0, late(s), 0))
    return pl.pallas_call(
        functools.partial(along_u_kernel, early),
        grid=(tiles + CELLS // GROUP,),
        out_shape=jax.ShapeDtypeStruct(shape, jnp.bfloat16),
        in_specs=[
            smem,
            smem,
            pl.BlockSpec(memory_space=pl.ANY),
            *in_specs,
            pl.BlockSpec((16, CELLS), lambda s: (soon(s), 0)),
            pl.BlockSpec((16, CELLS), lambda s: (soon(s), 0)),
            pl.BlockSpec((2 * ROWS, 2 * ROWS), lambda s: (0, 0)),
        ],
        out_specs=out_spec,
        scratch_shapes=[
            pltpu.VMEM((GROUP, GROUP, 2, 16, LANES), jnp.float32),
            pltpu.VMEM((2 * ROWS, CELLS * LANES), jnp.bfloat16),
        ],
        compiler_params=pltpu.CompilerParams(vmem_limit_bytes=VMEM_LIMIT),
        cost_estimate=pl.CostEstimate(flops=2 * 1024 * 2048 * 2048, bytes_accessed=8 << 20, transcendentals=0),
        name="u_first" if early else "u_last",
    )(place, w_value, after, *cells, tw_cos, tw_sin, jnp.asarray(short_table()))


def arrange_kernel(place_ref, *refs):
    one, (two_ref, rows_ref, cols_ref, out_ref, held) = refs[:-5], refs[-5:]
    q = lax.broadcasted_iota(jnp.int32, (LANES, BLOCK), 0)
    m = lax.broadcasted_iota(jnp.int32, (LANES, BLOCK), 1)
    total = None
    for shift in range(GROUP):
        j = lax.rem(place_ref[0] + GROUP - shift, GROUP)
        pick = jnp.where(m == GROUP * q + j, 1.0, 0.0).astype(jnp.bfloat16)
        other = [two_ref[0, r, j].astype(jnp.float32) + two_ref[1, r, j].astype(jnp.float32) for r in range(GROUP)]
        cells = (one[shift][...].astype(jnp.float32) + jnp.concatenate(other, axis=0)).astype(jnp.bfloat16)
        part = jnp.dot(cells, pick, preferred_element_type=jnp.float32)
        total = part if total is None else total + part
    total = total * (cols_ref[...] / NPIX)
    for part in range(GROUP):
        lanes = slice(part * LANES, (part + 1) * LANES)
        held[part] = total[:, lanes]
        for g in range(8):
            rows = slice(g * CELLS, (g + 1) * CELLS)
            out_ref[rows, lanes] = held[part, pl.ds(g, CELLS, 8), :] * rows_ref[rows, :]


def arrange(place, one, two, taper_rows, taper_cols):
    vmem = pl.BlockSpec(memory_space=pltpu.VMEM)
    return pl.pallas_call(
        arrange_kernel,
        out_shape=jax.ShapeDtypeStruct((8 * CELLS, BLOCK), jnp.float32),
        in_specs=[pl.BlockSpec(memory_space=pltpu.SMEM)] + [vmem] * (len(one) + 3),
        out_specs=vmem,
        scratch_shapes=[pltpu.VMEM((GROUP, 8 * CELLS, LANES), jnp.float32)],
        compiler_params=pltpu.CompilerParams(vmem_limit_bytes=VMEM_LIMIT),
        name="arrange",
    )(place, *one, two, taper_rows, taper_cols)


def columns_kernel(_, __, *refs):
    for cut, out in zip(refs[:GROUP], refs[GROUP:]):
        out[...] = cut[0]


def columns(grids, k, row, after):
    rows = 128
    cut = lambda n: pl.BlockSpec((1, rows, 2 * LANES), lambda s, place: (k, s, lax.rem(place[0] + n, GROUP)))
    return pl.pallas_call(
        columns_kernel,
        grid_spec=pltpu.PrefetchScalarGridSpec(
            num_scalar_prefetch=1,
            grid=(BLOCK // rows,),
            in_specs=[pl.BlockSpec(memory_space=pl.ANY)] + [cut(n) for n in range(GROUP)],
            out_specs=[pl.BlockSpec((rows, 2 * LANES), lambda s, place: (s, 0))] * GROUP,
        ),
        out_shape=[jax.ShapeDtypeStruct((BLOCK, 2 * LANES), grids.dtype)] * GROUP,
        name="columns",
    )(row, after, *[grids] * GROUP)


def around(blocks, axis, chains=()):
    before = {n: chain[i] for chain in chains for i, n in enumerate(chain[1:])}
    moved = {0: blocks[0]}
    for n in [n for chain in chains for n in chain] or range(1, GROUP):
        block = gate(blocks[n], moved[before[n]]) if n in before else blocks[n]
        moved[n] = lax.ppermute(block, axis, [(c, (c + n) % GROUP) for c in range(GROUP)])
    return [moved[-n % GROUP] for n in range(GROUP)]


def gate_kernel(*refs):
    del refs


def gate(value, *others):
    return pl.pallas_call(
        gate_kernel,
        out_shape=jax.ShapeDtypeStruct(value.shape, value.dtype),
        in_specs=[pl.BlockSpec(memory_space=pl.ANY)] * (1 + len(others)),
        out_specs=pl.BlockSpec(memory_space=pl.ANY),
        input_output_aliases={0: 0},
        name="gate",
    )(value, *others)


def swap(blocks, axes):
    return lax.all_to_all(blocks, axes, split_axis=0, concat_axis=0, tiled=True)


def on_device(grids, taper, w_steps):
    lay, row, col = lax.axis_index("layer"), lax.axis_index("row"), lax.axis_index("col")
    corner_u = (BLOCK * row + col).astype(jnp.int32).reshape(1)
    corner_v = (8 * CELLS * col + 8 * row).astype(jnp.int32).reshape(1)
    taper_cols = lax.dynamic_slice_in_dim(taper, BLOCK * row, BLOCK).reshape(1, BLOCK)
    taper_rows = lax.dynamic_slice_in_dim(taper, 8 * CELLS * (GROUP * lay + col), 8 * CELLS).reshape(8 * CELLS, 1)
    tables_u = [jnp.asarray(t) for t in row_tables()]
    tables_v = [jnp.asarray(t) for t in spread_tables()]
    own_u = [lax.dynamic_index_in_dim(t, row, 0, keepdims=False) for t in tables_u]
    own_v = [lax.dynamic_index_in_dim(t, col - col % 2, 0, keepdims=False) for t in tables_v]
    first_u, first_v = [t[0] for t in tables_u], [t[0] for t in tables_v]
    w_one, w_two = w_steps[:1], w_steps[1:]
    scalar = lambda value: value.astype(jnp.int32).reshape(1)

    side, place_y = col % 2, col // 2
    cells = grids.reshape(grids.shape[0], GROUP // 2, 2, ROWS, 2 * BLOCK)
    take = lambda k: lax.dynamic_slice(cells, (0, 0, k, 0, 0), (1, GROUP // 2, 1, ROWS, 2 * BLOCK))
    mine, give = (take(k).reshape(GROUP // 2, ROWS, 2 * BLOCK) for k in (side, 1 - side))
    got = lax.ppermute(give, "col", [(c, c ^ 1) for c in range(GROUP)])
    half = [None] * (GROUP // 2)
    for n in range(GROUP // 2):
        target = (place_y + n) % (GROUP // 2)
        block = jnp.stack([lax.dynamic_index_in_dim(t, target, 0, keepdims=False) for t in (mine, got)])
        last = block
        if n:
            block = lax.ppermute(block, "col", [(c, (c + 2 * n) % GROUP) for c in range(GROUP)])
        half[-n % (GROUP // 2)] = block
    other = around(columns(grids, 1, scalar(row), last), "row")
    half = along_v(True, half, *own_v, scalar(side), corner_v, w_one, w_one)
    half = gate(half, *other[1:])
    other = [block.reshape(GROUP, ROWS, 2 * LANES) for block in other]
    other = along_u(True, other, *own_u, corner_u, w_two, half)
    half = swap(half.reshape(CELLS, 2, ROWS, LANES), ("row", "col"))
    other = swap(other.reshape(CELLS, 2, ROWS, LANES), ("row", "col"))

    one = along_u(False, [half], *first_u, corner_u, w_one, w_one)
    two = along_v(False, [other.reshape(GROUP, GROUP, 2, ROWS, LANES)], *first_v, scalar(side), corner_v, w_two, one)
    one = one.reshape(LAYERS_AXIS, GROUP, 8 * CELLS, LANES)
    keep = lax.dynamic_index_in_dim(one, lay, 0, keepdims=False)
    send = lax.dynamic_index_in_dim(one, 1 - lay, 0, keepdims=False)
    send = lax.ppermute(send, "layer", [(0, 1), (1, 0)])
    one = (keep.astype(jnp.float32) + send.astype(jnp.float32)).astype(jnp.bfloat16)
    two = gate(two.reshape(LAYERS_AXIS * GROUP, GROUP, CELLS, LANES), one)
    two = swap(two, ("layer", "row")).reshape(LAYERS_AXIS, GROUP, GROUP, CELLS, LANES)
    one = [lax.dynamic_index_in_dim(one, (col + n) % GROUP, 0, keepdims=False) for n in range(GROUP)]
    one = around(one, "col")
    one = [one[-n % GROUP] for n in range(GROUP)]
    return arrange(scalar(col), one, two, taper_rows, taper_cols)


def solution(mesh):
    placed = (P("layer", "row", "col"), P(), P("layer"))
    return jax.shard_map(
        on_device, mesh=mesh, in_specs=placed, out_specs=P(("layer", "col"), "row"), check_vma=False
    )
```

```python
import functools
import math

import jax
import jax.numpy as jnp
import numpy as np
from jax import lax
from jax.experimental import pallas as pl
from jax.experimental.pallas import tpu as pltpu
from jax.sharding import PartitionSpec as P

INNER = 64
NPIX = 8192
LANES = 128
GROUP = 8
LAYERS_AXIS = 2
BLOCK = NPIX // GROUP
ROWS = BLOCK // GROUP
CELLS = NPIX // ROWS
HALF_ROOT = math.sqrt(0.5)
VMEM_LIMIT = 60 * 1024 * 1024


def power_terms(f):
    line = np.polynomial.Chebyshev.interpolate(lambda z: f(np.sqrt(z)), 4, domain=[0.0, 0.25])
    return [float(c) for c in line.convert(kind=np.polynomial.Polynomial).coef]


SIN_TERMS = power_terms(lambda t: np.pi * np.sinc(t))
COS_TERMS = power_terms(lambda t: np.cos(np.pi * t))


def unit(product, count):
    angle = 2.0 * np.pi / count * (product % count).astype(np.float64)
    return np.cos(angle), np.sin(angle)


def spread_tables():
    cell = np.arange(BLOCK) + BLOCK * np.arange(GROUP).reshape(GROUP, 1, 1)
    cosine, sine = unit(np.arange(GROUP)[:, None] * cell, NPIX)
    return cosine.astype(np.float32), sine.astype(np.float32)


def wide_tables():
    steps = np.arange(BLOCK)
    tables = unit(steps[:, None] * steps[None, :], BLOCK)
    return [np.ascontiguousarray(t.reshape(BLOCK, GROUP // 2, 2 * LANES).transpose(1, 0, 2)).astype(jnp.bfloat16) for t in tables]


def short_table():
    steps = np.arange(ROWS)
    cosine, sine = unit(steps[:, None] * steps[None, :], ROWS)
    upper = np.concatenate([cosine, -sine], axis=1)
    lower = np.concatenate([sine, cosine], axis=1)
    return np.concatenate([upper, lower], axis=0).astype(jnp.bfloat16)


def row_tables():
    start = np.arange(ROWS) + BLOCK * np.arange(GROUP)[:, None]
    cosine, sine = unit(start[:, :, None] * np.arange(CELLS), NPIX)
    return cosine.astype(np.float32), sine.astype(np.float32)


def eight(xr, xi, signs=None):
    er = [xr[c] + xr[c + 4] for c in range(4)]
    ei = [xi[c] + xi[c + 4] for c in range(4)]
    dr = [xr[c] - xr[c + 4] for c in range(4)]
    di = [xi[c] - xi[c + 4] for c in range(4)]
    if signs is not None:
        dr[1:], di[1:] = ([z * s for z, s in zip(d[1:], signs)] for d in (dr, di))
    evr, evi, odr, odi = er[0] + er[2], ei[0] + ei[2], er[1] + er[3], ei[1] + ei[3]
    nr, ni = (dr[1] - dr[3]) * HALF_ROOT, (di[1] - di[3]) * HALF_ROOT
    fr, fi = (dr[1] + dr[3]) * HALF_ROOT, (di[1] + di[3]) * HALF_ROOT
    outr, outi = [None] * 8, [None] * 8
    outr[0], outi[0] = evr + odr, evi + odi
    outr[4], outi[4] = evr - odr, evi - odi
    pairs = (
        (2, er[0] - er[2], ei[0] - ei[2], er[1] - er[3], ei[1] - ei[3]),
        (1, dr[0] + nr, di[0] + ni, dr[2] + fr, di[2] + fi),
        (3, dr[0] - nr, di[0] - ni, fr - dr[2], fi - di[2]),
    )
    for j, pr, pi, qr, qi in pairs:
        outr[j], outi[j] = pr - qi, pi + qr
        outr[8 - j], outi[8 - j] = pr + qi, pi - qr
    return outr, outi


def part_planes(pair):
    one, two = pair[:, :LANES].astype(jnp.float32), pair[:, LANES:].astype(jnp.float32)
    low = lax.broadcasted_iota(jnp.int32, one.shape, 1) < INNER
    real = jnp.where(low, one, pltpu.roll(two, INNER, 1))
    imag = jnp.where(low, pltpu.roll(one, INNER, 1), two)
    return real, imag


def screened(real, imag, l, m, w_value):
    across = (l.astype(jnp.float32) - NPIX / 2) / NPIX
    down = (m.astype(jnp.float32) - NPIX / 2) / NPIX
    square = 1.0 - across * across - down * down
    turns = w_value * (square * lax.rsqrt(square) - 1.0)
    t = turns - jnp.floor(turns + 0.5)
    t2 = t * t
    sine, cosine = SIN_TERMS[-1], COS_TERMS[-1]
    for a, b in zip(SIN_TERMS[-2::-1], COS_TERMS[-2::-1]):
        sine, cosine = sine * t2 + a, cosine * t2 + b
    sine = sine * t
    return real - 2.0 * sine * (sine * real + cosine * imag)


def along_v_kernel(early, core_ref, place_ref, w_ref, _, *refs):
    cells, (cos_ref, sin_ref, cos_table, sin_table, out_ref, spun) = refs[:-6], refs[-6:]
    step = pl.program_id(0)

    @pl.when(step == 0)
    def _():
        def one_tile(tile, carry):
            rows = pl.ds(pl.multiple_of(tile * 16, 16), 16)
            for part in range(GROUP):
                if early:
                    lanes = slice(2 * LANES * part, 2 * LANES * (part + 1))
                    pairs = [part_planes(ref[0, rows, lanes]) for ref in cells]
                    xr, xi = [p[0] for p in pairs], [p[1] for p in pairs]
                else:
                    xr = [cells[0][part, c, 0, rows].astype(jnp.float32) for c in range(GROUP)]
                    xi = [cells[0][part, c, 1, rows].astype(jnp.float32) for c in range(GROUP)]
                yr, yi = eight(xr, xi)
                lanes = slice(part * LANES, (part + 1) * LANES)
                for j in range(GROUP):
                    real, imag = yr[j], yi[j]
                    if j:
                        tc, ts = cos_ref[j : j + 1, lanes], sin_ref[j : j + 1, lanes]
                        real, imag = real * tc - imag * ts, real * ts + imag * tc
                    spun[j, 0, rows, lanes] = real.astype(jnp.bfloat16)
                    spun[j, 1, rows, lanes] = imag.astype(jnp.bfloat16)
            return carry

        lax.fori_loop(0, ROWS // 16, one_tile, 0)

    shape = (ROWS, LANES)
    row = lax.broadcasted_iota(jnp.int32, shape, 0)
    q = lax.broadcasted_iota(jnp.int32, shape, 1)
    def section(one, two):
        return jnp.dot(one, two[0], preferred_element_type=jnp.float32)

    for j in range(GROUP):
        both_real = section(spun[j, 0], cos_table) - section(spun[j, 1], sin_table)
        both_imag = section(spun[j, 0], sin_table) + section(spun[j, 1], cos_table)
        for half in range(2):
            real, imag = (z[:, half * LANES : (half + 1) * LANES] for z in (both_real, both_imag))
            if early:
                out_ref[half, j, 0] = real.astype(jnp.bfloat16)
                out_ref[half, j, 1] = imag.astype(jnp.bfloat16)
            else:
                l = row // CELLS * (NPIX // 2) + row % 8 * CELLS + row // 8 % 8 + place_ref[0]
                m = (2 * step + half) * BLOCK + GROUP * q + j
                image = screened(real, imag, l, m, w_ref[0].astype(jnp.float32)).astype(jnp.bfloat16)
                out_ref[0, half, j] = image[:CELLS]
                out_ref[1, half, j] = image[CELLS:]


def along_v(early, cells, tw_cos, tw_sin, core, place, w_value, after):
    whole = lambda *shape: pl.BlockSpec(shape, lambda s, core: (0,) * len(shape))
    smem = pl.BlockSpec(memory_space=pltpu.SMEM)
    if early:
        shape, block, index = (GROUP, GROUP, 2, ROWS, LANES), (2, GROUP, 2, ROWS, LANES), lambda s, core: (s, 0, 0, 0, 0)
        pick = lambda k: pl.BlockSpec((1, ROWS, 2 * BLOCK), lambda s, core: (lax.rem(core[0] + k, 2), 0, 0))
        in_specs = [pick(k) for _ in range(GROUP // 2) for k in range(2)]
        cells = [pair for pair in cells for _ in range(2)]
    else:
        shape, block = (LAYERS_AXIS, GROUP, GROUP, CELLS, LANES), (LAYERS_AXIS, 2, GROUP, CELLS, LANES)
        index = lambda s, core: (0, s, 0, 0, 0)
        in_specs = [whole(GROUP, GROUP, 2, ROWS, LANES)]
    return pl.pallas_call(
        functools.partial(along_v_kernel, early),
        out_shape=jax.ShapeDtypeStruct(shape, jnp.bfloat16),
        grid_spec=pltpu.PrefetchScalarGridSpec(
            num_scalar_prefetch=1,
            grid=(GROUP // 2,),
            in_specs=[
                smem,
                smem,
                pl.BlockSpec(memory_space=pl.ANY),
                *in_specs,
                whole(GROUP, BLOCK),
                whole(GROUP, BLOCK),
                *[pl.BlockSpec((1, BLOCK, 2 * LANES), lambda s, core: (s, 0, 0))] * 2,
            ],
            out_specs=pl.BlockSpec(block, index),
            scratch_shapes=[pltpu.VMEM((GROUP, 2, ROWS, BLOCK), jnp.bfloat16)],
        ),
        compiler_params=pltpu.CompilerParams(vmem_limit_bytes=VMEM_LIMIT),
        cost_estimate=pl.CostEstimate(flops=2 * 1024 * 2048 * 2048, bytes_accessed=16 << 20, transcendentals=0),
        name="v_first" if early else "v_last",
    )(core, place, w_value, after, *cells, tw_cos, tw_sin, *[jnp.asarray(t) for t in wide_tables()])


def along_u_kernel(early, place_ref, w_ref, _, *refs):
    cells, (cos_ref, sin_ref, table_ref, out_ref, mid, spun) = refs[:-6], refs[-6:]
    step = pl.program_id(0)
    tiles = ROWS // 16

    @pl.when(step < tiles)
    def _():
        for c in range(GROUP):
            if early:
                pairs = [part_planes(cells[r][c]) for r in range(GROUP)]
                xr, xi = [p[0] for p in pairs], [p[1] for p in pairs]
            else:
                xr = [cells[0][GROUP * r + c, 0].astype(jnp.float32) for r in range(GROUP)]
                xi = [cells[0][GROUP * r + c, 1].astype(jnp.float32) for r in range(GROUP)]
            place = lax.rem(w_ref[0], 4)
            yr, yi = eight(xr, xi, [jnp.where(place + n >= 4, -1.0, 1.0) for n in (1, 2, 3)] if early else None)
            for i in range(GROUP):
                wr, wi = math.cos(2 * math.pi * c * i / CELLS), math.sin(2 * math.pi * c * i / CELLS)
                if c * i == 0:
                    mid[i, c, 0], mid[i, c, 1] = yr[i], yi[i]
                else:
                    mid[i, c, 0] = yr[i] * wr - yi[i] * wi
                    mid[i, c, 1] = yr[i] * wi + yi[i] * wr
        rows = pl.ds(pl.multiple_of(step * 16, 16), 16)
        lower = pl.ds(pl.multiple_of(ROWS + step * 16, 16), 16)
        for i1 in range(GROUP):
            yr, yi = eight([mid[i1, c, 0] for c in range(GROUP)], [mid[i1, c, 1] for c in range(GROUP)])
            for i2 in range(GROUP):
                i = i1 + GROUP * i2
                tc, ts = cos_ref[:, i : i + 1], sin_ref[:, i : i + 1]
                lanes = slice(i * LANES, (i + 1) * LANES)
                spun[rows, lanes] = (yr[i2] * tc - yi[i2] * ts).astype(jnp.bfloat16)
                spun[lower, lanes] = (yr[i2] * ts + yi[i2] * tc).astype(jnp.bfloat16)

    @pl.when(step >= tiles)
    def _():
        block = step - tiles
        lanes = pl.ds(pl.multiple_of(block * GROUP * LANES, LANES), GROUP * LANES)
        full = jnp.dot(table_ref[...], spun[:, lanes], preferred_element_type=jnp.float32)
        shape = (ROWS, LANES)
        g = lax.broadcasted_iota(jnp.int32, shape, 0)
        m = place_ref[0] + GROUP * lax.broadcasted_iota(jnp.int32, shape, 1)

        def by_tile(first, second):
            both = [z.reshape(ROWS // 8, 8, LANES) for z in (first, second)]
            return jnp.concatenate(both, axis=1).astype(jnp.bfloat16)

        for n in range(0, GROUP, 2):
            real = [full[:ROWS, k * LANES : (k + 1) * LANES] for k in (n, n + 1)]
            imag = [full[ROWS:, k * LANES : (k + 1) * LANES] for k in (n, n + 1)]
            if early:
                for p, pair in enumerate((real, imag)):
                    both = by_tile(*pair)
                    for group in range(LAYERS_AXIS):
                        out_ref[0, :, p, group, 8 * n : 8 * n + 16, :] = both[GROUP * group : GROUP * (group + 1)]
            else:
                images = [
                    screened(real[k], imag[k], CELLS * g + (block * GROUP + n + k), m, w_ref[0].astype(jnp.float32))
                    for k in range(2)
                ]
                out_ref[:, 8 * n : 8 * n + 16, :] = by_tile(*images)


def along_u(early, cells, tw_cos, tw_sin, place, w_value, after):
    tiles = ROWS // 16
    late = lambda s: jnp.maximum(s - tiles, 0)
    soon = lambda s: jnp.minimum(s, tiles - 1)
    smem = pl.BlockSpec(memory_space=pltpu.SMEM)
    if early:
        in_specs = [pl.BlockSpec((GROUP, 16, 2 * LANES), lambda s: (0, soon(s), 0))] * GROUP
        shape = (GROUP, GROUP, 2, LAYERS_AXIS, CELLS, LANES)
        out_spec = pl.BlockSpec((1,) + shape[1:], lambda s: (late(s), 0, 0, 0, 0, 0))
    else:
        in_specs = [pl.BlockSpec((CELLS, 2, 16, LANES), lambda s: (0, 0, soon(s), 0))]
        shape = (ROWS // 8, 8 * CELLS, LANES)
        out_spec = pl.BlockSpec((ROWS // 8, 8 * GROUP, LANES), lambda s: (0, late(s), 0))
    return pl.pallas_call(
        functools.partial(along_u_kernel, early),
        grid=(tiles + CELLS // GROUP,),
        out_shape=jax.ShapeDtypeStruct(shape, jnp.bfloat16),
        in_specs=[
            smem,
            smem,
            pl.BlockSpec(memory_space=pl.ANY),
            *in_specs,
            pl.BlockSpec((16, CELLS), lambda s: (soon(s), 0)),
            pl.BlockSpec((16, CELLS), lambda s: (soon(s), 0)),
            pl.BlockSpec((2 * ROWS, 2 * ROWS), lambda s: (0, 0)),
        ],
        out_specs=out_spec,
        scratch_shapes=[
            pltpu.VMEM((GROUP, GROUP, 2, 16, LANES), jnp.float32),
            pltpu.VMEM((2 * ROWS, CELLS * LANES), jnp.bfloat16),
        ],
        compiler_params=pltpu.CompilerParams(vmem_limit_bytes=VMEM_LIMIT),
        cost_estimate=pl.CostEstimate(flops=2 * 1024 * 2048 * 2048, bytes_accessed=8 << 20, transcendentals=0),
        name="u_first" if early else "u_last",
    )(place, w_value, after, *cells, tw_cos, tw_sin, jnp.asarray(short_table()))


def arrange_kernel(place_ref, *refs):
    one, (two_ref, rows_ref, cols_ref, out_ref, held) = refs[:-5], refs[-5:]
    q = lax.broadcasted_iota(jnp.int32, (LANES, BLOCK), 0)
    m = lax.broadcasted_iota(jnp.int32, (LANES, BLOCK), 1)
    total = None
    for shift in range(GROUP):
        j = lax.rem(place_ref[0] // 2 + 4 - shift // 2, 4) * 2 + lax.rem(place_ref[0] + shift, 2)
        pick = jnp.where(m == GROUP * q + j, 1.0, 0.0).astype(jnp.bfloat16)
        other = [two_ref[0, r, j].astype(jnp.float32) + two_ref[1, r, j].astype(jnp.float32) for r in range(GROUP)]
        cells = (one[shift][...].astype(jnp.float32) + jnp.concatenate(other, axis=0)).astype(jnp.bfloat16)
        part = jnp.dot(cells, pick, preferred_element_type=jnp.float32)
        total = part if total is None else total + part
    total = total * (cols_ref[...] / NPIX)
    for part in range(GROUP):
        lanes = slice(part * LANES, (part + 1) * LANES)
        held[part] = total[:, lanes]
        for g in range(8):
            rows = slice(g * CELLS, (g + 1) * CELLS)
            out_ref[rows, lanes] = held[part, pl.ds(g, CELLS, 8), :] * rows_ref[rows, :]


def arrange(place, one, two, taper_rows, taper_cols):
    vmem = pl.BlockSpec(memory_space=pltpu.VMEM)
    return pl.pallas_call(
        arrange_kernel,
        out_shape=jax.ShapeDtypeStruct((8 * CELLS, BLOCK), jnp.float32),
        in_specs=[pl.BlockSpec(memory_space=pltpu.SMEM)] + [vmem] * (len(one) + 3),
        out_specs=vmem,
        scratch_shapes=[pltpu.VMEM((GROUP, 8 * CELLS, LANES), jnp.float32)],
        compiler_params=pltpu.CompilerParams(vmem_limit_bytes=VMEM_LIMIT),
        name="arrange",
    )(place, *one, two, taper_rows, taper_cols)


def columns_kernel(_, __, *refs):
    for cut, out in zip(refs[:GROUP], refs[GROUP:]):
        out[...] = cut[0]


def across_row(place, n):
    return (place // 4 + n // 4) % 2 * 4 + (place + n) % 4


def across_col(place, n):
    return (place // 2 + n // 2) % 4 * 2 + (place + n) % 2


def columns(grids, k, row, after):
    rows = 256
    cut = lambda n: pl.BlockSpec((1, rows, 2 * LANES), lambda s, place: (k, s, across_row(place[0], n)))
    return pl.pallas_call(
        columns_kernel,
        grid_spec=pltpu.PrefetchScalarGridSpec(
            num_scalar_prefetch=1,
            grid=(BLOCK // rows,),
            in_specs=[pl.BlockSpec(memory_space=pl.ANY)] + [cut(n) for n in range(GROUP)],
            out_specs=[pl.BlockSpec((rows, 2 * LANES), lambda s, place: (s, 0))] * GROUP,
        ),
        out_shape=[jax.ShapeDtypeStruct((BLOCK, 2 * LANES), grids.dtype)] * GROUP,
        compiler_params=pltpu.CompilerParams(vmem_limit_bytes=VMEM_LIMIT),
        name="columns",
    )(row, after, *[grids] * GROUP)


def around(blocks, axis, across, order):
    moved = {0: blocks[0]}
    for n in order:
        moved[n] = lax.ppermute(blocks[n], axis, [(c, across(c, n)) for c in range(GROUP)])
    return [moved[n] for n in range(GROUP)]


def gate_kernel(*refs):
    del refs


def gate(value, *others):
    return pl.pallas_call(
        gate_kernel,
        out_shape=jax.ShapeDtypeStruct(value.shape, value.dtype),
        in_specs=[pl.BlockSpec(memory_space=pl.ANY)] * (1 + len(others)),
        out_specs=pl.BlockSpec(memory_space=pl.ANY),
        input_output_aliases={0: 0},
        name="gate",
    )(value, *others)


def swap(blocks, axes):
    return lax.all_to_all(blocks, axes, split_axis=0, concat_axis=0, tiled=True)


def on_device(grids, taper, w_steps):
    lay, row, col = lax.axis_index("layer"), lax.axis_index("row"), lax.axis_index("col")
    corner_u = (BLOCK * row + col).astype(jnp.int32).reshape(1)
    corner_v = (8 * CELLS * col + 8 * row).astype(jnp.int32).reshape(1)
    taper_cols = lax.dynamic_slice_in_dim(taper, BLOCK * row, BLOCK).reshape(1, BLOCK)
    taper_rows = lax.dynamic_slice_in_dim(taper, 8 * CELLS * (GROUP * lay + col), 8 * CELLS).reshape(8 * CELLS, 1)
    tables_u = [jnp.asarray(t) for t in row_tables()]
    tables_v = [jnp.asarray(t) for t in spread_tables()]
    own_u = [lax.dynamic_index_in_dim(t, row, 0, keepdims=False) for t in tables_u]
    own_v = [lax.dynamic_index_in_dim(t, col - col % 2, 0, keepdims=False) for t in tables_v]
    first_u, first_v = [t[0] for t in tables_u], [t[0] for t in tables_v]
    w_one, w_two = w_steps[:1], w_steps[1:]
    scalar = lambda value: value.astype(jnp.int32).reshape(1)

    side, place_y = col % 2, col // 2
    cells = grids.reshape(grids.shape[0], GROUP // 2, 2, ROWS, 2 * BLOCK)
    take = lambda k: lax.dynamic_slice(cells, (0, 0, k, 0, 0), (1, GROUP // 2, 1, ROWS, 2 * BLOCK))
    mine, give = (take(k).reshape(GROUP // 2, ROWS, 2 * BLOCK) for k in (side, 1 - side))
    got = lax.ppermute(give, "col", [(c, c ^ 1) for c in range(GROUP)])
    half = [None] * (GROUP // 2)
    for n in range(GROUP // 2):
        target = (place_y + n) % (GROUP // 2)
        block = jnp.stack([lax.dynamic_index_in_dim(t, target, 0, keepdims=False) for t in (mine, got)])
        last = block
        if n:
            block = lax.ppermute(block, "col", [(c, (c + 2 * n) % GROUP) for c in range(GROUP)])
        half[-n % (GROUP // 2)] = block
    other = around(columns(grids, 1, scalar(row), last), "row", across_row, (3, 4, 5, 7, 6, 2, 1))
    half = along_v(True, half, *own_v, scalar(side), corner_v, w_one, w_one)
    half = gate(half, *other[1:])
    other = [other[n // 4 * 4 + -n % 4].reshape(GROUP, ROWS, 2 * LANES) for n in range(GROUP)]
    other = along_u(True, other, *own_u, corner_u, scalar(row), half)
    half = swap(half.reshape(CELLS, 2, ROWS, LANES), ("row", "col"))
    other = swap(other.reshape(CELLS, 2, ROWS, LANES), ("row", "col"))

    one = along_u(False, [half], *first_u, corner_u, w_one, w_one)
    two = along_v(False, [other.reshape(GROUP, GROUP, 2, ROWS, LANES)], *first_v, scalar(side), corner_v, w_two, one)
    one = one.reshape(LAYERS_AXIS, GROUP, 8 * CELLS, LANES)
    keep = lax.dynamic_index_in_dim(one, lay, 0, keepdims=False)
    send = lax.dynamic_index_in_dim(one, 1 - lay, 0, keepdims=False)
    send = lax.ppermute(send, "layer", [(0, 1), (1, 0)])
    one = (keep.astype(jnp.float32) + send.astype(jnp.float32)).astype(jnp.bfloat16)
    two = gate(two.reshape(LAYERS_AXIS * GROUP, GROUP, CELLS, LANES), one)
    two = swap(two, ("layer", "row")).reshape(LAYERS_AXIS, GROUP, GROUP, CELLS, LANES)
    one = [lax.dynamic_index_in_dim(one, across_col(col, n), 0, keepdims=False) for n in range(GROUP)]
    one = around(one, "col", across_col, (2, 3, 6, 7, 4, 5, 1))
    return arrange(scalar(col), one, two, taper_rows, taper_cols)


def solution(mesh):
    placed = (P("layer", "row", "col"), P(), P("layer"))
    return jax.shard_map(
        on_device, mesh=mesh, in_specs=placed, out_specs=P(("layer", "col"), "row"), check_vma=False
    )
```

```python
import functools
import math

import jax
import jax.numpy as jnp
import numpy as np
from jax import lax
from jax.experimental import pallas as pl
from jax.experimental.pallas import tpu as pltpu
from jax.sharding import PartitionSpec as P

INNER = 64
NPIX = 8192
LANES = 128
GROUP = 8
LAYERS_AXIS = 2
BLOCK = NPIX // GROUP
ROWS = BLOCK // GROUP
CELLS = NPIX // ROWS
HALF_ROOT = math.sqrt(0.5)
VMEM_LIMIT = 60 * 1024 * 1024


def power_terms(f):
    line = np.polynomial.Chebyshev.interpolate(lambda z: f(np.sqrt(z)), 4, domain=[0.0, 0.25])
    return [float(c) for c in line.convert(kind=np.polynomial.Polynomial).coef]


SIN_TERMS = power_terms(lambda t: np.pi * np.sinc(t))
COS_TERMS = power_terms(lambda t: np.cos(np.pi * t))


def unit(product, count):
    angle = 2.0 * np.pi / count * (product % count).astype(np.float64)
    return np.cos(angle), np.sin(angle)


def spread_tables():
    cell = np.arange(BLOCK) + BLOCK * np.arange(GROUP).reshape(GROUP, 1, 1)
    cosine, sine = unit(np.arange(GROUP)[:, None] * cell, NPIX)
    return cosine.astype(np.float32), sine.astype(np.float32)


def wide_tables():
    steps = np.arange(BLOCK)
    tables = unit(steps[:, None] * steps[None, :], BLOCK)
    return [np.ascontiguousarray(t.reshape(BLOCK, GROUP // 2, 2 * LANES).transpose(1, 0, 2)).astype(jnp.bfloat16) for t in tables]


def short_table():
    steps = np.arange(ROWS)
    cosine, sine = unit(steps[:, None] * steps[None, :], ROWS)
    upper = np.concatenate([cosine, -sine], axis=1)
    lower = np.concatenate([sine, cosine], axis=1)
    return np.concatenate([upper, lower], axis=0).astype(jnp.bfloat16)


def row_tables():
    start = np.arange(ROWS) + BLOCK * np.arange(GROUP)[:, None]
    cosine, sine = unit(start[:, :, None] * np.arange(CELLS), NPIX)
    return cosine.astype(np.float32), sine.astype(np.float32)


def eight(xr, xi, signs=None):
    er = [xr[c] + xr[c + 4] for c in range(4)]
    ei = [xi[c] + xi[c + 4] for c in range(4)]
    dr = [xr[c] - xr[c + 4] for c in range(4)]
    di = [xi[c] - xi[c + 4] for c in range(4)]
    if signs is not None:
        dr[1:], di[1:] = ([z * s for z, s in zip(d[1:], signs)] for d in (dr, di))
    evr, evi, odr, odi = er[0] + er[2], ei[0] + ei[2], er[1] + er[3], ei[1] + ei[3]
    nr, ni = (dr[1] - dr[3]) * HALF_ROOT, (di[1] - di[3]) * HALF_ROOT
    fr, fi = (dr[1] + dr[3]) * HALF_ROOT, (di[1] + di[3]) * HALF_ROOT
    outr, outi = [None] * 8, [None] * 8
    outr[0], outi[0] = evr + odr, evi + odi
    outr[4], outi[4] = evr - odr, evi - odi
    pairs = (
        (2, er[0] - er[2], ei[0] - ei[2], er[1] - er[3], ei[1] - ei[3]),
        (1, dr[0] + nr, di[0] + ni, dr[2] + fr, di[2] + fi),
        (3, dr[0] - nr, di[0] - ni, fr - dr[2], fi - di[2]),
    )
    for j, pr, pi, qr, qi in pairs:
        outr[j], outi[j] = pr - qi, pi + qr
        outr[8 - j], outi[8 - j] = pr + qi, pi - qr
    return outr, outi


def part_planes(pair):
    one, two = pair[:, :LANES].astype(jnp.float32), pair[:, LANES:].astype(jnp.float32)
    low = lax.broadcasted_iota(jnp.int32, one.shape, 1) < INNER
    real = jnp.where(low, one, pltpu.roll(two, INNER, 1))
    imag = jnp.where(low, pltpu.roll(one, INNER, 1), two)
    return real, imag


def screened(real, imag, l, m, w_value):
    across = (l.astype(jnp.float32) - NPIX / 2) / NPIX
    down = (m.astype(jnp.float32) - NPIX / 2) / NPIX
    square = 1.0 - across * across - down * down
    turns = w_value * (square * lax.rsqrt(square) - 1.0)
    t = turns - jnp.floor(turns + 0.5)
    t2 = t * t
    sine, cosine = SIN_TERMS[-1], COS_TERMS[-1]
    for a, b in zip(SIN_TERMS[-2::-1], COS_TERMS[-2::-1]):
        sine, cosine = sine * t2 + a, cosine * t2 + b
    sine = sine * t
    return real - 2.0 * sine * (sine * real + cosine * imag)


def along_v_kernel(early, core_ref, place_ref, w_ref, _, *refs):
    cells, (cos_ref, sin_ref, cos_table, sin_table, out_ref, spun) = refs[:-6], refs[-6:]
    step = pl.program_id(0)

    @pl.when(step == 0)
    def _():
        def one_tile(tile, carry):
            rows = pl.ds(pl.multiple_of(tile * 16, 16), 16)
            for part in range(GROUP):
                if early:
                    lanes = slice(2 * LANES * part, 2 * LANES * (part + 1))
                    pairs = [part_planes(ref[0, rows, lanes]) for ref in cells]
                    xr, xi = [p[0] for p in pairs], [p[1] for p in pairs]
                else:
                    xr = [cells[0][part, c, 0, rows].astype(jnp.float32) for c in range(GROUP)]
                    xi = [cells[0][part, c, 1, rows].astype(jnp.float32) for c in range(GROUP)]
                yr, yi = eight(xr, xi)
                lanes = slice(part * LANES, (part + 1) * LANES)
                for j in range(GROUP):
                    real, imag = yr[j], yi[j]
                    if j:
                        tc, ts = cos_ref[j : j + 1, lanes], sin_ref[j : j + 1, lanes]
                        real, imag = real * tc - imag * ts, real * ts + imag * tc
                    spun[j, 0, rows, lanes] = real.astype(jnp.bfloat16)
                    spun[j, 1, rows, lanes] = imag.astype(jnp.bfloat16)
            return carry

        lax.fori_loop(0, ROWS // 16, one_tile, 0)

    shape = (ROWS, LANES)
    row = lax.broadcasted_iota(jnp.int32, shape, 0)
    q = lax.broadcasted_iota(jnp.int32, shape, 1)
    def section(one, two):
        return jnp.dot(one, two[0], preferred_element_type=jnp.float32)

    for j in range(GROUP):
        both_real = section(spun[j, 0], cos_table) - section(spun[j, 1], sin_table)
        both_imag = section(spun[j, 0], sin_table) + section(spun[j, 1], cos_table)
        for half in range(2):
            real, imag = (z[:, half * LANES : (half + 1) * LANES] for z in (both_real, both_imag))
            if early:
                out_ref[half, j, 0] = real.astype(jnp.bfloat16)
                out_ref[half, j, 1] = imag.astype(jnp.bfloat16)
            else:
                l = row // CELLS * (NPIX // 2) + row % 8 * CELLS + row // 8 % 8 + place_ref[0]
                m = (2 * step + half) * BLOCK + GROUP * q + j
                image = screened(real, imag, l, m, w_ref[0].astype(jnp.float32)).astype(jnp.bfloat16)
                out_ref[0, half, j] = image[:CELLS]
                out_ref[1, half, j] = image[CELLS:]


def along_v(early, cells, tw_cos, tw_sin, core, place, w_value, after):
    whole = lambda *shape: pl.BlockSpec(shape, lambda s, core: (0,) * len(shape))
    smem = pl.BlockSpec(memory_space=pltpu.SMEM)
    if early:
        shape, block, index = (GROUP, GROUP, 2, ROWS, LANES), (2, GROUP, 2, ROWS, LANES), lambda s, core: (s, 0, 0, 0, 0)
        pick = lambda k: pl.BlockSpec((1, ROWS, 2 * BLOCK), lambda s, core: (lax.rem(core[0] + k, 2), 0, 0))
        in_specs = [pick(k) for _ in range(GROUP // 2) for k in range(2)]
        cells = [pair for pair in cells for _ in range(2)]
    else:
        shape, block = (LAYERS_AXIS, GROUP, GROUP, CELLS, LANES), (LAYERS_AXIS, 2, GROUP, CELLS, LANES)
        index = lambda s, core: (0, s, 0, 0, 0)
        in_specs = [whole(GROUP, GROUP, 2, ROWS, LANES)]
    return pl.pallas_call(
        functools.partial(along_v_kernel, early),
        out_shape=jax.ShapeDtypeStruct(shape, jnp.bfloat16),
        grid_spec=pltpu.PrefetchScalarGridSpec(
            num_scalar_prefetch=1,
            grid=(GROUP // 2,),
            in_specs=[
                smem,
                smem,
                pl.BlockSpec(memory_space=pl.ANY),
                *in_specs,
                whole(GROUP, BLOCK),
                whole(GROUP, BLOCK),
                *[pl.BlockSpec((1, BLOCK, 2 * LANES), lambda s, core: (s, 0, 0))] * 2,
            ],
            out_specs=pl.BlockSpec(block, index),
            scratch_shapes=[pltpu.VMEM((GROUP, 2, ROWS, BLOCK), jnp.bfloat16)],
        ),
        compiler_params=pltpu.CompilerParams(vmem_limit_bytes=VMEM_LIMIT),
        cost_estimate=pl.CostEstimate(flops=2 * 1024 * 2048 * 2048, bytes_accessed=16 << 20, transcendentals=0),
        name="v_first" if early else "v_last",
    )(core, place, w_value, after, *cells, tw_cos, tw_sin, *[jnp.asarray(t) for t in wide_tables()])


def along_u_kernel(early, place_ref, w_ref, _, *refs):
    cells, (cos_ref, sin_ref, table_ref, out_ref, mid, spun) = refs[:-6], refs[-6:]
    step = pl.program_id(0)
    tiles = ROWS // 16

    @pl.when(step < tiles)
    def _():
        for c in range(GROUP):
            if early:
                pairs = [part_planes(cells[r][c]) for r in range(GROUP)]
                xr, xi = [p[0] for p in pairs], [p[1] for p in pairs]
            else:
                xr = [cells[0][GROUP * r + c, 0].astype(jnp.float32) for r in range(GROUP)]
                xi = [cells[0][GROUP * r + c, 1].astype(jnp.float32) for r in range(GROUP)]
            place = lax.rem(w_ref[0], 4)
            yr, yi = eight(xr, xi, [jnp.where(place + n >= 4, -1.0, 1.0) for n in (1, 2, 3)] if early else None)
            for i in range(GROUP):
                wr, wi = math.cos(2 * math.pi * c * i / CELLS), math.sin(2 * math.pi * c * i / CELLS)
                if c * i == 0:
                    mid[i, c, 0], mid[i, c, 1] = yr[i], yi[i]
                else:
                    mid[i, c, 0] = yr[i] * wr - yi[i] * wi
                    mid[i, c, 1] = yr[i] * wi + yi[i] * wr
        rows = pl.ds(pl.multiple_of(step * 16, 16), 16)
        lower = pl.ds(pl.multiple_of(ROWS + step * 16, 16), 16)
        for i1 in range(GROUP):
            yr, yi = eight([mid[i1, c, 0] for c in range(GROUP)], [mid[i1, c, 1] for c in range(GROUP)])
            for i2 in range(GROUP):
                i = i1 + GROUP * i2
                tc, ts = cos_ref[:, i : i + 1], sin_ref[:, i : i + 1]
                lanes = slice(i * LANES, (i + 1) * LANES)
                spun[rows, lanes] = (yr[i2] * tc - yi[i2] * ts).astype(jnp.bfloat16)
                spun[lower, lanes] = (yr[i2] * ts + yi[i2] * tc).astype(jnp.bfloat16)

    @pl.when(step >= tiles)
    def _():
        block = step - tiles
        lanes = pl.ds(pl.multiple_of(block * GROUP * LANES, LANES), GROUP * LANES)
        full = jnp.dot(table_ref[...], spun[:, lanes], preferred_element_type=jnp.float32)
        shape = (ROWS, LANES)
        g = lax.broadcasted_iota(jnp.int32, shape, 0)
        m = place_ref[0] + GROUP * lax.broadcasted_iota(jnp.int32, shape, 1)

        def by_tile(first, second):
            both = [z.reshape(ROWS // 8, 8, LANES) for z in (first, second)]
            return jnp.concatenate(both, axis=1).astype(jnp.bfloat16)

        for n in range(0, GROUP, 2):
            real = [full[:ROWS, k * LANES : (k + 1) * LANES] for k in (n, n + 1)]
            imag = [full[ROWS:, k * LANES : (k + 1) * LANES] for k in (n, n + 1)]
            if early:
                for p, pair in enumerate((real, imag)):
                    both = by_tile(*pair)
                    for group in range(LAYERS_AXIS):
                        out_ref[0, :, p, group, 8 * n : 8 * n + 16, :] = both[GROUP * group : GROUP * (group + 1)]
            else:
                images = [
                    screened(real[k], imag[k], CELLS * g + (block * GROUP + n + k), m, w_ref[0].astype(jnp.float32))
                    for k in range(2)
                ]
                out_ref[:, 8 * n : 8 * n + 16, :] = by_tile(*images)


def along_u(early, cells, tw_cos, tw_sin, place, w_value, after):
    tiles = ROWS // 16
    late = lambda s: jnp.maximum(s - tiles, 0)
    soon = lambda s: jnp.minimum(s, tiles - 1)
    smem = pl.BlockSpec(memory_space=pltpu.SMEM)
    if early:
        in_specs = [pl.BlockSpec((GROUP, 16, 2 * LANES), lambda s: (0, soon(s), 0))] * GROUP
        shape = (GROUP, GROUP, 2, LAYERS_AXIS, CELLS, LANES)
        out_spec = pl.BlockSpec((1,) + shape[1:], lambda s: (late(s), 0, 0, 0, 0, 0))
    else:
        in_specs = [pl.BlockSpec((CELLS, 2, 16, LANES), lambda s: (0, 0, soon(s), 0))]
        shape = (ROWS // 8, 8 * CELLS, LANES)
        out_spec = pl.BlockSpec((ROWS // 8, 8 * GROUP, LANES), lambda s: (0, late(s), 0))
    return pl.pallas_call(
        functools.partial(along_u_kernel, early),
        grid=(tiles + CELLS // GROUP,),
        out_shape=jax.ShapeDtypeStruct(shape, jnp.bfloat16),
        in_specs=[
            smem,
            smem,
            pl.BlockSpec(memory_space=pl.ANY),
            *in_specs,
            pl.BlockSpec((16, CELLS), lambda s: (soon(s), 0)),
            pl.BlockSpec((16, CELLS), lambda s: (soon(s), 0)),
            pl.BlockSpec((2 * ROWS, 2 * ROWS), lambda s: (0, 0)),
        ],
        out_specs=out_spec,
        scratch_shapes=[
            pltpu.VMEM((GROUP, GROUP, 2, 16, LANES), jnp.float32),
            pltpu.VMEM((2 * ROWS, CELLS * LANES), jnp.bfloat16),
        ],
        compiler_params=pltpu.CompilerParams(vmem_limit_bytes=VMEM_LIMIT),
        cost_estimate=pl.CostEstimate(flops=2 * 1024 * 2048 * 2048, bytes_accessed=8 << 20, transcendentals=0),
        name="u_first" if early else "u_last",
    )(place, w_value, after, *cells, tw_cos, tw_sin, jnp.asarray(short_table()))


def arrange_kernel(place_ref, *refs):
    one, (two_ref, rows_ref, cols_ref, out_ref, held) = refs[:-5], refs[-5:]
    q = lax.broadcasted_iota(jnp.int32, (LANES, BLOCK), 0)
    m = lax.broadcasted_iota(jnp.int32, (LANES, BLOCK), 1)
    total = None
    for shift in range(GROUP):
        j = lax.rem(place_ref[0] // 2 + 4 - shift // 2, 4) * 2 + lax.rem(place_ref[0] + shift, 2)
        pick = jnp.where(m == GROUP * q + j, 1.0, 0.0).astype(jnp.bfloat16)
        other = [two_ref[0, r, j].astype(jnp.float32) + two_ref[1, r, j].astype(jnp.float32) for r in range(GROUP)]
        cells = (one[shift][...].astype(jnp.float32) + jnp.concatenate(other, axis=0)).astype(jnp.bfloat16)
        part = jnp.dot(cells, pick, preferred_element_type=jnp.float32)
        total = part if total is None else total + part
    total = total * (cols_ref[...] / NPIX)
    for part in range(GROUP):
        lanes = slice(part * LANES, (part + 1) * LANES)
        held[part] = total[:, lanes]
        for g in range(8):
            rows = slice(g * CELLS, (g + 1) * CELLS)
            out_ref[rows, lanes] = held[part, pl.ds(g, CELLS, 8), :] * rows_ref[rows, :]


def arrange(place, one, two, taper_rows, taper_cols):
    vmem = pl.BlockSpec(memory_space=pltpu.VMEM)
    return pl.pallas_call(
        arrange_kernel,
        out_shape=jax.ShapeDtypeStruct((8 * CELLS, BLOCK), jnp.float32),
        in_specs=[pl.BlockSpec(memory_space=pltpu.SMEM)] + [vmem] * (len(one) + 3),
        out_specs=vmem,
        scratch_shapes=[pltpu.VMEM((GROUP, 8 * CELLS, LANES), jnp.float32)],
        compiler_params=pltpu.CompilerParams(vmem_limit_bytes=VMEM_LIMIT),
        name="arrange",
    )(place, *one, two, taper_rows, taper_cols)


def columns_kernel(_, __, *refs):
    for cut, out in zip(refs[:GROUP], refs[GROUP:]):
        out[...] = cut[0]


def across_row(place, n):
    return (place // 4 + n // 4) % 2 * 4 + (place + n) % 4


def across_col(place, n):
    return (place // 2 + n // 2) % 4 * 2 + (place + n) % 2


def columns(grids, k, row, after):
    rows = 256
    cut = lambda n: pl.BlockSpec((1, rows, 2 * LANES), lambda s, place: (k, s, across_row(place[0], n)))
    return pl.pallas_call(
        columns_kernel,
        grid_spec=pltpu.PrefetchScalarGridSpec(
            num_scalar_prefetch=1,
            grid=(BLOCK // rows,),
            in_specs=[pl.BlockSpec(memory_space=pl.ANY)] + [cut(n) for n in range(GROUP)],
            out_specs=[pl.BlockSpec((rows, 2 * LANES), lambda s, place: (s, 0))] * GROUP,
        ),
        out_shape=[jax.ShapeDtypeStruct((BLOCK, 2 * LANES), grids.dtype)] * GROUP,
        compiler_params=pltpu.CompilerParams(vmem_limit_bytes=VMEM_LIMIT),
        name="columns",
    )(row, after, *[grids] * GROUP)


def around(blocks, axis, across, order):
    moved = {0: blocks[0]}
    for n in order:
        moved[n] = lax.ppermute(blocks[n], axis, [(c, across(c, n)) for c in range(GROUP)])
    return [moved[n] for n in range(GROUP)]


def gate_kernel(*refs):
    del refs


def gate(value, *others):
    return pl.pallas_call(
        gate_kernel,
        out_shape=jax.ShapeDtypeStruct(value.shape, value.dtype),
        in_specs=[pl.BlockSpec(memory_space=pl.ANY)] * (1 + len(others)),
        out_specs=pl.BlockSpec(memory_space=pl.ANY),
        input_output_aliases={0: 0},
        name="gate",
    )(value, *others)


def swap(blocks, axes):
    return lax.all_to_all(blocks, axes, split_axis=0, concat_axis=0, tiled=True)


def on_device(grids, taper, w_steps):
    lay, row, col = lax.axis_index("layer"), lax.axis_index("row"), lax.axis_index("col")
    corner_u = (BLOCK * row + col).astype(jnp.int32).reshape(1)
    corner_v = (8 * CELLS * col + 8 * row).astype(jnp.int32).reshape(1)
    taper_cols = lax.dynamic_slice_in_dim(taper, BLOCK * row, BLOCK).reshape(1, BLOCK)
    taper_rows = lax.dynamic_slice_in_dim(taper, 8 * CELLS * (GROUP * lay + col), 8 * CELLS).reshape(8 * CELLS, 1)
    tables_u = [jnp.asarray(t) for t in row_tables()]
    tables_v = [jnp.asarray(t) for t in spread_tables()]
    own_u = [lax.dynamic_index_in_dim(t, row, 0, keepdims=False) for t in tables_u]
    own_v = [lax.dynamic_index_in_dim(t, col - col % 2, 0, keepdims=False) for t in tables_v]
    first_u, first_v = [t[0] for t in tables_u], [t[0] for t in tables_v]
    w_one, w_two = w_steps[:1], w_steps[1:]
    scalar = lambda value: value.astype(jnp.int32).reshape(1)

    side, place_y = col % 2, col // 2
    cells = grids.reshape(grids.shape[0], GROUP // 2, 2, ROWS, 2 * BLOCK)
    take = lambda k: lax.dynamic_slice(cells, (0, 0, k, 0, 0), (1, GROUP // 2, 1, ROWS, 2 * BLOCK))
    mine, give = (take(k).reshape(GROUP // 2, ROWS, 2 * BLOCK) for k in (side, 1 - side))
    got = lax.ppermute(give, "col", [(c, c ^ 1) for c in range(GROUP)])
    half = {}

    def along_y(n, *earlier):
        target = (place_y + n) % (GROUP // 2)
        block = jnp.stack([lax.dynamic_index_in_dim(t, target, 0, keepdims=False) for t in (mine, got)])
        if earlier:
            block = gate(block, *earlier)
        moved = lax.ppermute(block, "col", [(c, (c + 2 * n) % GROUP) for c in range(GROUP)]) if n else block
        half[-n % (GROUP // 2)] = moved
        return block

    along_y(1)
    begun = along_y(3)
    other = around(columns(grids, 1, scalar(row), begun), "row", across_row, (1, 3, 4, 5, 7, 2, 6))
    along_y(2, half[1], half[3], other[1], other[3], other[4])
    along_y(0)
    half = [half[n] for n in range(GROUP // 2)]
    half = along_v(True, half, *own_v, scalar(side), corner_v, w_one, w_one)
    half = gate(half, *other[1:])
    other = [other[n // 4 * 4 + -n % 4].reshape(GROUP, ROWS, 2 * LANES) for n in range(GROUP)]
    other = along_u(True, other, *own_u, corner_u, scalar(row), half)
    half = swap(half.reshape(CELLS, 2, ROWS, LANES), ("row", "col"))
    other = swap(other.reshape(CELLS, 2, ROWS, LANES), ("row", "col"))

    one = along_u(False, [half], *first_u, corner_u, w_one, w_one)
    two = along_v(False, [other.reshape(GROUP, GROUP, 2, ROWS, LANES)], *first_v, scalar(side), corner_v, w_two, one)
    one = one.reshape(LAYERS_AXIS, GROUP, 8 * CELLS, LANES)
    keep = lax.dynamic_index_in_dim(one, lay, 0, keepdims=False)
    send = lax.dynamic_index_in_dim(one, 1 - lay, 0, keepdims=False)
    send = lax.ppermute(send, "layer", [(0, 1), (1, 0)])
    one = (keep.astype(jnp.float32) + send.astype(jnp.float32)).astype(jnp.bfloat16)
    two = gate(two.reshape(LAYERS_AXIS * GROUP, GROUP, CELLS, LANES), one)
    two = swap(two, ("layer", "row")).reshape(LAYERS_AXIS, GROUP, GROUP, CELLS, LANES)
    one = [lax.dynamic_index_in_dim(one, across_col(col, n), 0, keepdims=False) for n in range(GROUP)]
    one = around(one, "col", across_col, (2, 3, 6, 7, 4, 5, 1))
    return arrange(scalar(col), one, two, taper_rows, taper_cols)


def solution(mesh):
    placed = (P("layer", "row", "col"), P(), P("layer"))
    return jax.shard_map(
        on_device, mesh=mesh, in_specs=placed, out_specs=P(("layer", "col"), "row"), check_vma=False
    )
```

```python
import functools
import math

import jax
import jax.numpy as jnp
import numpy as np
from jax import lax
from jax.experimental import pallas as pl
from jax.experimental.pallas import tpu as pltpu
from jax.sharding import PartitionSpec as P

INNER = 64
NPIX = 8192
LANES = 128
GROUP = 8
LAYERS_AXIS = 2
BLOCK = NPIX // GROUP
ROWS = BLOCK // GROUP
CELLS = NPIX // ROWS
HALF_ROOT = math.sqrt(0.5)
VMEM_LIMIT = 60 * 1024 * 1024


def power_terms(f):
    line = np.polynomial.Chebyshev.interpolate(lambda z: f(np.sqrt(z)), 4, domain=[0.0, 0.25])
    return [float(c) for c in line.convert(kind=np.polynomial.Polynomial).coef]


SIN_TERMS = power_terms(lambda t: np.pi * np.sinc(t))
COS_TERMS = power_terms(lambda t: np.cos(np.pi * t))


def unit(product, count):
    angle = 2.0 * np.pi / count * (product % count).astype(np.float64)
    return np.cos(angle), np.sin(angle)


def spread_tables():
    cell = np.arange(BLOCK) + BLOCK * np.arange(GROUP).reshape(GROUP, 1, 1)
    cosine, sine = unit(np.arange(GROUP)[:, None] * cell, NPIX)
    return cosine.astype(np.float32), sine.astype(np.float32)


def wide_tables():
    steps = np.arange(BLOCK)
    tables = unit(steps[:, None] * steps[None, :], BLOCK)
    return [np.ascontiguousarray(t.reshape(BLOCK, GROUP // 2, 2 * LANES).transpose(1, 0, 2)).astype(jnp.bfloat16) for t in tables]


def short_table():
    steps = np.arange(ROWS)
    cosine, sine = unit(steps[:, None] * steps[None, :], ROWS)
    upper = np.concatenate([cosine, -sine], axis=1)
    lower = np.concatenate([sine, cosine], axis=1)
    return np.concatenate([upper, lower], axis=0).astype(jnp.bfloat16)


def row_tables():
    start = np.arange(ROWS) + BLOCK * np.arange(GROUP)[:, None]
    cosine, sine = unit(start[:, :, None] * np.arange(CELLS), NPIX)
    return cosine.astype(np.float32), sine.astype(np.float32)


def eight(xr, xi, signs=None):
    er = [xr[c] + xr[c + 4] for c in range(4)]
    ei = [xi[c] + xi[c + 4] for c in range(4)]
    dr = [xr[c] - xr[c + 4] for c in range(4)]
    di = [xi[c] - xi[c + 4] for c in range(4)]
    if signs is not None:
        dr[1:], di[1:] = ([z * s for z, s in zip(d[1:], signs)] for d in (dr, di))
    evr, evi, odr, odi = er[0] + er[2], ei[0] + ei[2], er[1] + er[3], ei[1] + ei[3]
    nr, ni = (dr[1] - dr[3]) * HALF_ROOT, (di[1] - di[3]) * HALF_ROOT
    fr, fi = (dr[1] + dr[3]) * HALF_ROOT, (di[1] + di[3]) * HALF_ROOT
    outr, outi = [None] * 8, [None] * 8
    outr[0], outi[0] = evr + odr, evi + odi
    outr[4], outi[4] = evr - odr, evi - odi
    pairs = (
        (2, er[0] - er[2], ei[0] - ei[2], er[1] - er[3], ei[1] - ei[3]),
        (1, dr[0] + nr, di[0] + ni, dr[2] + fr, di[2] + fi),
        (3, dr[0] - nr, di[0] - ni, fr - dr[2], fi - di[2]),
    )
    for j, pr, pi, qr, qi in pairs:
        outr[j], outi[j] = pr - qi, pi + qr
        outr[8 - j], outi[8 - j] = pr + qi, pi - qr
    return outr, outi


def part_planes(pair):
    one, two = pair[:, :LANES].astype(jnp.float32), pair[:, LANES:].astype(jnp.float32)
    low = lax.broadcasted_iota(jnp.int32, one.shape, 1) < INNER
    real = jnp.where(low, one, pltpu.roll(two, INNER, 1))
    imag = jnp.where(low, pltpu.roll(one, INNER, 1), two)
    return real, imag


def screened(real, imag, l, m, w_value):
    across = (l.astype(jnp.float32) - NPIX / 2) / NPIX
    down = (m.astype(jnp.float32) - NPIX / 2) / NPIX
    square = 1.0 - across * across - down * down
    turns = w_value * (square * lax.rsqrt(square) - 1.0)
    t = turns - jnp.floor(turns + 0.5)
    t2 = t * t
    sine, cosine = SIN_TERMS[-1], COS_TERMS[-1]
    for a, b in zip(SIN_TERMS[-2::-1], COS_TERMS[-2::-1]):
        sine, cosine = sine * t2 + a, cosine * t2 + b
    sine = sine * t
    return real - 2.0 * sine * (sine * real + cosine * imag)


def along_v_kernel(early, core_ref, place_ref, w_ref, _, *refs):
    cells, (cos_ref, sin_ref, cos_table, sin_table, out_ref, spun) = refs[:-6], refs[-6:]
    step = pl.program_id(0)

    @pl.when(step == 0)
    def _():
        def one_tile(tile, carry):
            rows = pl.ds(pl.multiple_of(tile * 16, 16), 16)
            for part in range(GROUP):
                if early:
                    lanes = slice(2 * LANES * part, 2 * LANES * (part + 1))
                    pairs = [part_planes(ref[0, rows, lanes]) for ref in cells]
                    xr, xi = [p[0] for p in pairs], [p[1] for p in pairs]
                else:
                    xr = [cells[0][part, c, 0, rows].astype(jnp.float32) for c in range(GROUP)]
                    xi = [cells[0][part, c, 1, rows].astype(jnp.float32) for c in range(GROUP)]
                yr, yi = eight(xr, xi)
                lanes = slice(part * LANES, (part + 1) * LANES)
                for j in range(GROUP):
                    real, imag = yr[j], yi[j]
                    if j:
                        tc, ts = cos_ref[j : j + 1, lanes], sin_ref[j : j + 1, lanes]
                        real, imag = real * tc - imag * ts, real * ts + imag * tc
                    spun[j, 0, rows, lanes] = real.astype(jnp.bfloat16)
                    spun[j, 1, rows, lanes] = imag.astype(jnp.bfloat16)
            return carry

        lax.fori_loop(0, ROWS // 16, one_tile, 0)

    shape = (ROWS, LANES)
    row = lax.broadcasted_iota(jnp.int32, shape, 0)
    q = lax.broadcasted_iota(jnp.int32, shape, 1)
    def section(one, two):
        return jnp.dot(one, two[0], preferred_element_type=jnp.float32)

    for j in range(GROUP):
        both_real = section(spun[j, 0], cos_table) - section(spun[j, 1], sin_table)
        both_imag = section(spun[j, 0], sin_table) + section(spun[j, 1], cos_table)
        for half in range(2):
            real, imag = (z[:, half * LANES : (half + 1) * LANES] for z in (both_real, both_imag))
            if early:
                out_ref[half, j, 0] = real.astype(jnp.bfloat16)
                out_ref[half, j, 1] = imag.astype(jnp.bfloat16)
            else:
                l = row // CELLS * (NPIX // 2) + row % 8 * CELLS + row // 8 % 8 + place_ref[0]
                m = (2 * step + half) * BLOCK + GROUP * q + j
                image = screened(real, imag, l, m, w_ref[0].astype(jnp.float32)).astype(jnp.bfloat16)
                out_ref[0, half, j] = image[:CELLS]
                out_ref[1, half, j] = image[CELLS:]


def along_v(early, cells, tw_cos, tw_sin, core, place, w_value, after):
    whole = lambda *shape: pl.BlockSpec(shape, lambda s, core: (0,) * len(shape))
    smem = pl.BlockSpec(memory_space=pltpu.SMEM)
    if early:
        shape, block, index = (GROUP, GROUP, 2, ROWS, LANES), (2, GROUP, 2, ROWS, LANES), lambda s, core: (s, 0, 0, 0, 0)
        pick = lambda k: pl.BlockSpec((1, ROWS, 2 * BLOCK), lambda s, core: (lax.rem(core[0] + k, 2), 0, 0))
        in_specs = [pick(k) for _ in range(GROUP // 2) for k in range(2)]
        cells = [pair for pair in cells for _ in range(2)]
    else:
        shape, block = (LAYERS_AXIS, GROUP, GROUP, CELLS, LANES), (LAYERS_AXIS, 2, GROUP, CELLS, LANES)
        index = lambda s, core: (0, s, 0, 0, 0)
        in_specs = [whole(GROUP, GROUP, 2, ROWS, LANES)]
    return pl.pallas_call(
        functools.partial(along_v_kernel, early),
        out_shape=jax.ShapeDtypeStruct(shape, jnp.bfloat16),
        grid_spec=pltpu.PrefetchScalarGridSpec(
            num_scalar_prefetch=1,
            grid=(GROUP // 2,),
            in_specs=[
                smem,
                smem,
                pl.BlockSpec(memory_space=pl.ANY),
                *in_specs,
                whole(GROUP, BLOCK),
                whole(GROUP, BLOCK),
                *[pl.BlockSpec((1, BLOCK, 2 * LANES), lambda s, core: (s, 0, 0))] * 2,
            ],
            out_specs=pl.BlockSpec(block, index),
            scratch_shapes=[pltpu.VMEM((GROUP, 2, ROWS, BLOCK), jnp.bfloat16)],
        ),
        compiler_params=pltpu.CompilerParams(vmem_limit_bytes=VMEM_LIMIT),
        cost_estimate=pl.CostEstimate(flops=2 * 1024 * 2048 * 2048, bytes_accessed=16 << 20, transcendentals=0),
        name="v_first" if early else "v_last",
    )(core, place, w_value, after, *cells, tw_cos, tw_sin, *[jnp.asarray(t) for t in wide_tables()])


def along_u_kernel(early, place_ref, w_ref, _, *refs):
    cells, (cos_ref, sin_ref, table_ref, out_ref, mid, spun) = refs[:-6], refs[-6:]
    step = pl.program_id(0)
    tiles = ROWS // 16

    @pl.when(step < tiles)
    def _():
        for c in range(GROUP):
            if early:
                pairs = [part_planes(cells[r][c]) for r in range(GROUP)]
                xr, xi = [p[0] for p in pairs], [p[1] for p in pairs]
            else:
                xr = [cells[0][GROUP * r + c, 0].astype(jnp.float32) for r in range(GROUP)]
                xi = [cells[0][GROUP * r + c, 1].astype(jnp.float32) for r in range(GROUP)]
            place = lax.rem(w_ref[0], 4)
            yr, yi = eight(xr, xi, [jnp.where(place + n >= 4, -1.0, 1.0) for n in (1, 2, 3)] if early else None)
            for i in range(GROUP):
                wr, wi = math.cos(2 * math.pi * c * i / CELLS), math.sin(2 * math.pi * c * i / CELLS)
                if c * i == 0:
                    mid[i, c, 0], mid[i, c, 1] = yr[i], yi[i]
                else:
                    mid[i, c, 0] = yr[i] * wr - yi[i] * wi
                    mid[i, c, 1] = yr[i] * wi + yi[i] * wr
        rows = pl.ds(pl.multiple_of(step * 16, 16), 16)
        lower = pl.ds(pl.multiple_of(ROWS + step * 16, 16), 16)
        for i1 in range(GROUP):
            yr, yi = eight([mid[i1, c, 0] for c in range(GROUP)], [mid[i1, c, 1] for c in range(GROUP)])
            for i2 in range(GROUP):
                i = i1 + GROUP * i2
                tc, ts = cos_ref[:, i : i + 1], sin_ref[:, i : i + 1]
                lanes = slice(i * LANES, (i + 1) * LANES)
                spun[rows, lanes] = (yr[i2] * tc - yi[i2] * ts).astype(jnp.bfloat16)
                spun[lower, lanes] = (yr[i2] * ts + yi[i2] * tc).astype(jnp.bfloat16)

    @pl.when(step >= tiles)
    def _():
        block = step - tiles
        lanes = pl.ds(pl.multiple_of(block * GROUP * LANES, LANES), GROUP * LANES)
        full = jnp.dot(table_ref[...], spun[:, lanes], preferred_element_type=jnp.float32)
        shape = (ROWS, LANES)
        g = lax.broadcasted_iota(jnp.int32, shape, 0)
        m = place_ref[0] + GROUP * lax.broadcasted_iota(jnp.int32, shape, 1)

        def by_tile(first, second):
            both = [z.reshape(ROWS // 8, 8, LANES) for z in (first, second)]
            return jnp.concatenate(both, axis=1).astype(jnp.bfloat16)

        for n in range(0, GROUP, 2):
            real = [full[:ROWS, k * LANES : (k + 1) * LANES] for k in (n, n + 1)]
            imag = [full[ROWS:, k * LANES : (k + 1) * LANES] for k in (n, n + 1)]
            if early:
                for p, pair in enumerate((real, imag)):
                    both = by_tile(*pair)
                    for group in range(LAYERS_AXIS):
                        out_ref[0, :, p, group, 8 * n : 8 * n + 16, :] = both[GROUP * group : GROUP * (group + 1)]
            else:
                images = [
                    screened(real[k], imag[k], CELLS * g + (block * GROUP + n + k), m, w_ref[0].astype(jnp.float32))
                    for k in range(2)
                ]
                out_ref[:, 8 * n : 8 * n + 16, :] = by_tile(*images)


def along_u(early, cells, tw_cos, tw_sin, place, w_value, after):
    tiles = ROWS // 16
    late = lambda s: jnp.maximum(s - tiles, 0)
    soon = lambda s: jnp.minimum(s, tiles - 1)
    smem = pl.BlockSpec(memory_space=pltpu.SMEM)
    if early:
        in_specs = [pl.BlockSpec((GROUP, 16, 2 * LANES), lambda s: (0, soon(s), 0))] * GROUP
        shape = (GROUP, GROUP, 2, LAYERS_AXIS, CELLS, LANES)
        out_spec = pl.BlockSpec((1,) + shape[1:], lambda s: (late(s), 0, 0, 0, 0, 0))
    else:
        in_specs = [pl.BlockSpec((CELLS, 2, 16, LANES), lambda s: (0, 0, soon(s), 0))]
        shape = (ROWS // 8, 8 * CELLS, LANES)
        out_spec = pl.BlockSpec((ROWS // 8, 8 * GROUP, LANES), lambda s: (0, late(s), 0))
    return pl.pallas_call(
        functools.partial(along_u_kernel, early),
        grid=(tiles + CELLS // GROUP,),
        out_shape=jax.ShapeDtypeStruct(shape, jnp.bfloat16),
        in_specs=[
            smem,
            smem,
            pl.BlockSpec(memory_space=pl.ANY),
            *in_specs,
            pl.BlockSpec((16, CELLS), lambda s: (soon(s), 0)),
            pl.BlockSpec((16, CELLS), lambda s: (soon(s), 0)),
            pl.BlockSpec((2 * ROWS, 2 * ROWS), lambda s: (0, 0)),
        ],
        out_specs=out_spec,
        scratch_shapes=[
            pltpu.VMEM((GROUP, GROUP, 2, 16, LANES), jnp.float32),
            pltpu.VMEM((2 * ROWS, CELLS * LANES), jnp.bfloat16),
        ],
        compiler_params=pltpu.CompilerParams(vmem_limit_bytes=VMEM_LIMIT),
        cost_estimate=pl.CostEstimate(flops=2 * 1024 * 2048 * 2048, bytes_accessed=8 << 20, transcendentals=0),
        name="u_first" if early else "u_last",
    )(place, w_value, after, *cells, tw_cos, tw_sin, jnp.asarray(short_table()))


def arrange_kernel(place_ref, *refs):
    one, (two_ref, rows_ref, cols_ref, out_ref, held) = refs[:-5], refs[-5:]
    q = lax.broadcasted_iota(jnp.int32, (LANES, BLOCK), 0)
    m = lax.broadcasted_iota(jnp.int32, (LANES, BLOCK), 1)
    total = None
    for shift in range(GROUP):
        j = lax.rem(place_ref[0] // 2 + 4 - shift // 2, 4) * 2 + lax.rem(place_ref[0] + shift, 2)
        pick = jnp.where(m == GROUP * q + j, 1.0, 0.0).astype(jnp.bfloat16)
        other = [two_ref[0, r, j].astype(jnp.float32) + two_ref[1, r, j].astype(jnp.float32) for r in range(GROUP)]
        cells = (one[shift][...].astype(jnp.float32) + jnp.concatenate(other, axis=0)).astype(jnp.bfloat16)
        part = jnp.dot(cells, pick, preferred_element_type=jnp.float32)
        total = part if total is None else total + part
    total = total * (cols_ref[...] / NPIX)
    for part in range(GROUP):
        lanes = slice(part * LANES, (part + 1) * LANES)
        held[part] = total[:, lanes]
        for g in range(8):
            rows = slice(g * CELLS, (g + 1) * CELLS)
            out_ref[rows, lanes] = held[part, pl.ds(g, CELLS, 8), :] * rows_ref[rows, :]


def arrange(place, one, two, taper_rows, taper_cols):
    vmem = pl.BlockSpec(memory_space=pltpu.VMEM)
    return pl.pallas_call(
        arrange_kernel,
        out_shape=jax.ShapeDtypeStruct((8 * CELLS, BLOCK), jnp.float32),
        in_specs=[pl.BlockSpec(memory_space=pltpu.SMEM)] + [vmem] * (len(one) + 3),
        out_specs=vmem,
        scratch_shapes=[pltpu.VMEM((GROUP, 8 * CELLS, LANES), jnp.float32)],
        compiler_params=pltpu.CompilerParams(vmem_limit_bytes=VMEM_LIMIT),
        name="arrange",
    )(place, *one, two, taper_rows, taper_cols)


def columns_kernel(_, __, *refs):
    for cut, out in zip(refs[:GROUP], refs[GROUP:]):
        out[...] = cut[0]


def across_row(place, n):
    return (place // 4 + n // 4) % 2 * 4 + (place + n) % 4


def across_col(place, n):
    return (place // 2 + n // 2) % 4 * 2 + (place + n) % 2


def columns(grids, k, row, after):
    rows = 256
    cut = lambda n: pl.BlockSpec((1, rows, 2 * LANES), lambda s, place: (k, s, across_row(place[0], n)))
    return pl.pallas_call(
        columns_kernel,
        grid_spec=pltpu.PrefetchScalarGridSpec(
            num_scalar_prefetch=1,
            grid=(BLOCK // rows,),
            in_specs=[pl.BlockSpec(memory_space=pl.ANY)] + [cut(n) for n in range(GROUP)],
            out_specs=[pl.BlockSpec((rows, 2 * LANES), lambda s, place: (s, 0))] * GROUP,
        ),
        out_shape=[jax.ShapeDtypeStruct((BLOCK, 2 * LANES), grids.dtype)] * GROUP,
        compiler_params=pltpu.CompilerParams(vmem_limit_bytes=VMEM_LIMIT),
        name="columns",
    )(row, after, *[grids] * GROUP)


def around(blocks, axis, across, order):
    moved = {0: blocks[0]}
    for n in order:
        moved[n] = lax.ppermute(blocks[n], axis, [(c, across(c, n)) for c in range(GROUP)])
    return [moved[n] for n in range(GROUP)]


def gate_kernel(*refs):
    del refs


def gate(value, *others):
    return pl.pallas_call(
        gate_kernel,
        out_shape=jax.ShapeDtypeStruct(value.shape, value.dtype),
        in_specs=[pl.BlockSpec(memory_space=pl.ANY)] * (1 + len(others)),
        out_specs=pl.BlockSpec(memory_space=pl.ANY),
        input_output_aliases={0: 0},
        name="gate",
    )(value, *others)


def swap(blocks, axes):
    return lax.all_to_all(blocks, axes, split_axis=0, concat_axis=0, tiled=True)


def on_device(grids, taper, w_steps):
    lay, row, col = lax.axis_index("layer"), lax.axis_index("row"), lax.axis_index("col")
    corner_u = (BLOCK * row + col).astype(jnp.int32).reshape(1)
    corner_v = (8 * CELLS * col + 8 * row).astype(jnp.int32).reshape(1)
    taper_cols = lax.dynamic_slice_in_dim(taper, BLOCK * row, BLOCK).reshape(1, BLOCK)
    taper_rows = lax.dynamic_slice_in_dim(taper, 8 * CELLS * (GROUP * lay + col), 8 * CELLS).reshape(8 * CELLS, 1)
    tables_u = [jnp.asarray(t) for t in row_tables()]
    tables_v = [jnp.asarray(t) for t in spread_tables()]
    own_u = [lax.dynamic_index_in_dim(t, row, 0, keepdims=False) for t in tables_u]
    own_v = [lax.dynamic_index_in_dim(t, col - col % 2, 0, keepdims=False) for t in tables_v]
    first_u, first_v = [t[0] for t in tables_u], [t[0] for t in tables_v]
    w_one, w_two = w_steps[:1], w_steps[1:]
    scalar = lambda value: value.astype(jnp.int32).reshape(1)

    side, place_y = col % 2, col // 2
    cells = grids.reshape(grids.shape[0], GROUP // 2, 2, ROWS, 2 * BLOCK)
    take = lambda k: lax.dynamic_slice(cells, (0, 0, k, 0, 0), (1, GROUP // 2, 1, ROWS, 2 * BLOCK))
    mine, give = (take(k).reshape(GROUP // 2, ROWS, 2 * BLOCK) for k in (side, 1 - side))
    got = lax.ppermute(give, "col", [(c, c ^ 1) for c in range(GROUP)])
    half = {}

    def along_y(n, *earlier):
        target = (place_y + n) % (GROUP // 2)
        block = jnp.stack([lax.dynamic_index_in_dim(t, target, 0, keepdims=False) for t in (mine, got)])
        if earlier:
            block = gate(block, *earlier)
        moved = lax.ppermute(block, "col", [(c, (c + 2 * n) % GROUP) for c in range(GROUP)]) if n else block
        half[-n % (GROUP // 2)] = moved
        return block

    along_y(1)
    begun = along_y(3)
    other = around(columns(grids, 1, scalar(row), begun), "row", across_row, (1, 3, 4, 5, 7, 2, 6))
    along_y(2, half[1], half[3], other[1], other[3], other[4])
    along_y(0)
    half = [half[n] for n in range(GROUP // 2)]
    half = along_v(True, half, *own_v, scalar(side), corner_v, w_one, w_one)
    half = gate(half, *other[1:])
    other = [other[n // 4 * 4 + -n % 4].reshape(GROUP, ROWS, 2 * LANES) for n in range(GROUP)]
    other = along_u(True, other, *own_u, corner_u, scalar(row), half)
    half = swap(half.reshape(CELLS, 2, ROWS, LANES), ("row", "col"))
    other = swap(other.reshape(CELLS, 2, ROWS, LANES), ("row", "col"))

    one = along_u(False, [half], *first_u, corner_u, w_one, w_one)
    two = along_v(False, [other.reshape(GROUP, GROUP, 2, ROWS, LANES)], *first_v, scalar(side), corner_v, w_two, one)
    one = one.reshape(LAYERS_AXIS, GROUP, 8 * CELLS, LANES)
    keep = lax.dynamic_index_in_dim(one, lay, 0, keepdims=False)
    send = lax.dynamic_index_in_dim(one, 1 - lay, 0, keepdims=False)
    send = lax.ppermute(send, "layer", [(0, 1), (1, 0)])
    two = gate(two.reshape(LAYERS_AXIS * GROUP, GROUP, CELLS, LANES), send)
    one = (keep.astype(jnp.float32) + send.astype(jnp.float32)).astype(jnp.bfloat16)
    two = swap(two, ("layer", "row")).reshape(LAYERS_AXIS, GROUP, GROUP, CELLS, LANES)
    one = [lax.dynamic_index_in_dim(one, across_col(col, n), 0, keepdims=False) for n in range(GROUP)]
    one = around(one, "col", across_col, (2, 3, 6, 7, 4, 5, 1))
    return arrange(scalar(col), one, two, taper_rows, taper_cols)


def solution(mesh):
    placed = (P("layer", "row", "col"), P(), P("layer"))
    return jax.shard_map(
        on_device, mesh=mesh, in_specs=placed, out_specs=P(("layer", "col"), "row"), check_vma=False
    )
```

```python
import functools
import math

import jax
import jax.numpy as jnp
import numpy as np
from jax import lax
from jax.experimental import pallas as pl
from jax.experimental.pallas import tpu as pltpu
from jax.sharding import PartitionSpec as P

INNER = 64
NPIX = 8192
LANES = 128
GROUP = 8
LAYERS_AXIS = 2
BLOCK = NPIX // GROUP
ROWS = BLOCK // GROUP
CELLS = NPIX // ROWS
HALF_ROOT = math.sqrt(0.5)
VMEM_LIMIT = 60 * 1024 * 1024


def power_terms(f):
    line = np.polynomial.Chebyshev.interpolate(lambda z: f(np.sqrt(z)), 4, domain=[0.0, 0.25])
    return [float(c) for c in line.convert(kind=np.polynomial.Polynomial).coef]


SIN_TERMS = power_terms(lambda t: np.pi * np.sinc(t))
COS_TERMS = power_terms(lambda t: np.cos(np.pi * t))


def unit(product, count):
    angle = 2.0 * np.pi / count * (product % count).astype(np.float64)
    return np.cos(angle), np.sin(angle)


def spread_tables():
    cell = np.arange(BLOCK) + BLOCK * np.arange(GROUP).reshape(GROUP, 1, 1)
    cosine, sine = unit(np.arange(GROUP)[:, None] * cell, NPIX)
    return cosine.astype(np.float32), sine.astype(np.float32)


def wide_tables():
    steps = np.arange(BLOCK)
    tables = unit(steps[:, None] * steps[None, :], BLOCK)
    return [np.ascontiguousarray(t.reshape(BLOCK, GROUP // 2, 2 * LANES).transpose(1, 0, 2)).astype(jnp.bfloat16) for t in tables]


def short_table():
    steps = np.arange(ROWS)
    cosine, sine = unit(steps[:, None] * steps[None, :], ROWS)
    upper = np.concatenate([cosine, -sine], axis=1)
    lower = np.concatenate([sine, cosine], axis=1)
    return np.concatenate([upper, lower], axis=0).astype(jnp.bfloat16)


def row_tables():
    start = np.arange(ROWS) + BLOCK * np.arange(GROUP)[:, None]
    cosine, sine = unit(start[:, :, None] * np.arange(CELLS), NPIX)
    return cosine.astype(np.float32), sine.astype(np.float32)


def eight(xr, xi, signs=None):
    er = [xr[c] + xr[c + 4] for c in range(4)]
    ei = [xi[c] + xi[c + 4] for c in range(4)]
    dr = [xr[c] - xr[c + 4] for c in range(4)]
    di = [xi[c] - xi[c + 4] for c in range(4)]
    if signs is not None:
        dr[1:], di[1:] = ([z * s for z, s in zip(d[1:], signs)] for d in (dr, di))
    evr, evi, odr, odi = er[0] + er[2], ei[0] + ei[2], er[1] + er[3], ei[1] + ei[3]
    nr, ni = (dr[1] - dr[3]) * HALF_ROOT, (di[1] - di[3]) * HALF_ROOT
    fr, fi = (dr[1] + dr[3]) * HALF_ROOT, (di[1] + di[3]) * HALF_ROOT
    outr, outi = [None] * 8, [None] * 8
    outr[0], outi[0] = evr + odr, evi + odi
    outr[4], outi[4] = evr - odr, evi - odi
    pairs = (
        (2, er[0] - er[2], ei[0] - ei[2], er[1] - er[3], ei[1] - ei[3]),
        (1, dr[0] + nr, di[0] + ni, dr[2] + fr, di[2] + fi),
        (3, dr[0] - nr, di[0] - ni, fr - dr[2], fi - di[2]),
    )
    for j, pr, pi, qr, qi in pairs:
        outr[j], outi[j] = pr - qi, pi + qr
        outr[8 - j], outi[8 - j] = pr + qi, pi - qr
    return outr, outi


def part_planes(pair):
    one, two = pair[:, :LANES].astype(jnp.float32), pair[:, LANES:].astype(jnp.float32)
    low = lax.broadcasted_iota(jnp.int32, one.shape, 1) < INNER
    real = jnp.where(low, one, pltpu.roll(two, INNER, 1))
    imag = jnp.where(low, pltpu.roll(one, INNER, 1), two)
    return real, imag


def screened(real, imag, l, m, w_value):
    across = (l.astype(jnp.float32) - NPIX / 2) / NPIX
    down = (m.astype(jnp.float32) - NPIX / 2) / NPIX
    square = 1.0 - across * across - down * down
    turns = w_value * (square * lax.rsqrt(square) - 1.0)
    t = turns - jnp.floor(turns + 0.5)
    t2 = t * t
    sine, cosine = SIN_TERMS[-1], COS_TERMS[-1]
    for a, b in zip(SIN_TERMS[-2::-1], COS_TERMS[-2::-1]):
        sine, cosine = sine * t2 + a, cosine * t2 + b
    sine = sine * t
    return real - 2.0 * sine * (sine * real + cosine * imag)


def along_v_kernel(early, core_ref, place_ref, w_ref, _, *refs):
    cells, (cos_ref, sin_ref, cos_table, sin_table, out_ref, spun) = refs[:-6], refs[-6:]
    step = pl.program_id(0)

    @pl.when(step == 0)
    def _():
        def one_tile(tile, carry):
            rows = pl.ds(pl.multiple_of(tile * 16, 16), 16)
            for part in range(GROUP):
                if early:
                    lanes = slice(2 * LANES * part, 2 * LANES * (part + 1))
                    pairs = [part_planes(ref[0, rows, lanes]) for ref in cells]
                    xr, xi = [p[0] for p in pairs], [p[1] for p in pairs]
                else:
                    xr = [cells[0][part, c, 0, rows].astype(jnp.float32) for c in range(GROUP)]
                    xi = [cells[0][part, c, 1, rows].astype(jnp.float32) for c in range(GROUP)]
                yr, yi = eight(xr, xi)
                lanes = slice(part * LANES, (part + 1) * LANES)
                for j in range(GROUP):
                    real, imag = yr[j], yi[j]
                    if j:
                        tc, ts = cos_ref[j : j + 1, lanes], sin_ref[j : j + 1, lanes]
                        real, imag = real * tc - imag * ts, real * ts + imag * tc
                    spun[j, 0, rows, lanes] = real.astype(jnp.bfloat16)
                    spun[j, 1, rows, lanes] = imag.astype(jnp.bfloat16)
            return carry

        lax.fori_loop(0, ROWS // 16, one_tile, 0)

    shape = (ROWS, LANES)
    row = lax.broadcasted_iota(jnp.int32, shape, 0)
    q = lax.broadcasted_iota(jnp.int32, shape, 1)
    def section(one, two):
        return jnp.dot(one, two[0], preferred_element_type=jnp.float32)

    for j in range(GROUP):
        both_real = section(spun[j, 0], cos_table) - section(spun[j, 1], sin_table)
        both_imag = section(spun[j, 0], sin_table) + section(spun[j, 1], cos_table)
        for half in range(2):
            real, imag = (z[:, half * LANES : (half + 1) * LANES] for z in (both_real, both_imag))
            if early:
                out_ref[half, j, 0] = real.astype(jnp.bfloat16)
                out_ref[half, j, 1] = imag.astype(jnp.bfloat16)
            else:
                l = row // CELLS * (NPIX // 2) + row % 8 * CELLS + row // 8 % 8 + place_ref[0]
                m = (2 * step + half) * BLOCK + GROUP * q + j
                image = screened(real, imag, l, m, w_ref[0].astype(jnp.float32)).astype(jnp.bfloat16)
                out_ref[0, half, j] = image[:CELLS]
                out_ref[1, half, j] = image[CELLS:]


def along_v(early, cells, tw_cos, tw_sin, core, place, w_value, after):
    whole = lambda *shape: pl.BlockSpec(shape, lambda s, core: (0,) * len(shape))
    smem = pl.BlockSpec(memory_space=pltpu.SMEM)
    if early:
        shape, block, index = (GROUP, GROUP, 2, ROWS, LANES), (2, GROUP, 2, ROWS, LANES), lambda s, core: (s, 0, 0, 0, 0)
        pick = lambda k: pl.BlockSpec((1, ROWS, 2 * BLOCK), lambda s, core: (lax.rem(core[0] + k, 2), 0, 0))
        in_specs = [pick(k) for _ in range(GROUP // 2) for k in range(2)]
        cells = [pair for pair in cells for _ in range(2)]
    else:
        shape, block = (LAYERS_AXIS, GROUP, GROUP, CELLS, LANES), (LAYERS_AXIS, 2, GROUP, CELLS, LANES)
        index = lambda s, core: (0, s, 0, 0, 0)
        in_specs = [whole(GROUP, GROUP, 2, ROWS, LANES)]
    return pl.pallas_call(
        functools.partial(along_v_kernel, early),
        out_shape=jax.ShapeDtypeStruct(shape, jnp.bfloat16),
        grid_spec=pltpu.PrefetchScalarGridSpec(
            num_scalar_prefetch=1,
            grid=(GROUP // 2,),
            in_specs=[
                smem,
                smem,
                pl.BlockSpec(memory_space=pl.ANY),
                *in_specs,
                whole(GROUP, BLOCK),
                whole(GROUP, BLOCK),
                *[pl.BlockSpec((1, BLOCK, 2 * LANES), lambda s, core: (s, 0, 0))] * 2,
            ],
            out_specs=pl.BlockSpec(block, index),
            scratch_shapes=[pltpu.VMEM((GROUP, 2, ROWS, BLOCK), jnp.bfloat16)],
        ),
        compiler_params=pltpu.CompilerParams(vmem_limit_bytes=VMEM_LIMIT),
        cost_estimate=pl.CostEstimate(flops=2 * 1024 * 2048 * 2048, bytes_accessed=16 << 20, transcendentals=0),
        name="v_first" if early else "v_last",
    )(core, place, w_value, after, *cells, tw_cos, tw_sin, *[jnp.asarray(t) for t in wide_tables()])


def along_u_kernel(early, place_ref, w_ref, _, *refs):
    cells, (cos_ref, sin_ref, table_ref, out_ref, mid, spun) = refs[:-6], refs[-6:]
    step = pl.program_id(0)
    tiles = ROWS // 16

    @pl.when(step < tiles)
    def _():
        for c in range(GROUP):
            if early:
                pairs = [part_planes(cells[r][c]) for r in range(GROUP)]
                xr, xi = [p[0] for p in pairs], [p[1] for p in pairs]
            else:
                xr = [cells[0][GROUP * r + c, 0].astype(jnp.float32) for r in range(GROUP)]
                xi = [cells[0][GROUP * r + c, 1].astype(jnp.float32) for r in range(GROUP)]
            place = lax.rem(w_ref[0], 4)
            yr, yi = eight(xr, xi, [jnp.where(place + n >= 4, -1.0, 1.0) for n in (1, 2, 3)] if early else None)
            for i in range(GROUP):
                wr, wi = math.cos(2 * math.pi * c * i / CELLS), math.sin(2 * math.pi * c * i / CELLS)
                if c * i == 0:
                    mid[i, c, 0], mid[i, c, 1] = yr[i], yi[i]
                else:
                    mid[i, c, 0] = yr[i] * wr - yi[i] * wi
                    mid[i, c, 1] = yr[i] * wi + yi[i] * wr
        rows = pl.ds(pl.multiple_of(step * 16, 16), 16)
        lower = pl.ds(pl.multiple_of(ROWS + step * 16, 16), 16)
        for i1 in range(GROUP):
            yr, yi = eight([mid[i1, c, 0] for c in range(GROUP)], [mid[i1, c, 1] for c in range(GROUP)])
            for i2 in range(GROUP):
                i = i1 + GROUP * i2
                tc, ts = cos_ref[:, i : i + 1], sin_ref[:, i : i + 1]
                lanes = slice(i * LANES, (i + 1) * LANES)
                spun[rows, lanes] = (yr[i2] * tc - yi[i2] * ts).astype(jnp.bfloat16)
                spun[lower, lanes] = (yr[i2] * ts + yi[i2] * tc).astype(jnp.bfloat16)

    @pl.when(step >= tiles)
    def _():
        block = step - tiles
        lanes = pl.ds(pl.multiple_of(block * GROUP * LANES, LANES), GROUP * LANES)
        full = jnp.dot(table_ref[...], spun[:, lanes], preferred_element_type=jnp.float32)
        shape = (ROWS, LANES)
        g = lax.broadcasted_iota(jnp.int32, shape, 0)
        m = place_ref[0] + GROUP * lax.broadcasted_iota(jnp.int32, shape, 1)

        def by_tile(first, second):
            both = [z.reshape(ROWS // 8, 8, LANES) for z in (first, second)]
            return jnp.concatenate(both, axis=1).astype(jnp.bfloat16)

        for n in range(0, GROUP, 2):
            real = [full[:ROWS, k * LANES : (k + 1) * LANES] for k in (n, n + 1)]
            imag = [full[ROWS:, k * LANES : (k + 1) * LANES] for k in (n, n + 1)]
            if early:
                for p, pair in enumerate((real, imag)):
                    both = by_tile(*pair)
                    for group in range(LAYERS_AXIS):
                        out_ref[0, :, p, group, 8 * n : 8 * n + 16, :] = both[GROUP * group : GROUP * (group + 1)]
            else:
                images = [
                    screened(real[k], imag[k], CELLS * g + (block * GROUP + n + k), m, w_ref[0].astype(jnp.float32))
                    for k in range(2)
                ]
                out_ref[:, 8 * n : 8 * n + 16, :] = by_tile(*images)


def along_u(early, cells, tw_cos, tw_sin, place, w_value, after):
    tiles = ROWS // 16
    late = lambda s: jnp.maximum(s - tiles, 0)
    soon = lambda s: jnp.minimum(s, tiles - 1)
    smem = pl.BlockSpec(memory_space=pltpu.SMEM)
    if early:
        in_specs = [pl.BlockSpec((GROUP, 16, 2 * LANES), lambda s: (0, soon(s), 0))] * GROUP
        shape = (GROUP, GROUP, 2, LAYERS_AXIS, CELLS, LANES)
        out_spec = pl.BlockSpec((1,) + shape[1:], lambda s: (late(s), 0, 0, 0, 0, 0))
    else:
        in_specs = [pl.BlockSpec((CELLS, 2, 16, LANES), lambda s: (0, 0, soon(s), 0))]
        shape = (ROWS // 8, 8 * CELLS, LANES)
        out_spec = pl.BlockSpec((ROWS // 8, 8 * GROUP, LANES), lambda s: (0, late(s), 0))
    return pl.pallas_call(
        functools.partial(along_u_kernel, early),
        grid=(tiles + CELLS // GROUP,),
        out_shape=jax.ShapeDtypeStruct(shape, jnp.bfloat16),
        in_specs=[
            smem,
            smem,
            pl.BlockSpec(memory_space=pl.ANY),
            *in_specs,
            pl.BlockSpec((16, CELLS), lambda s: (soon(s), 0)),
            pl.BlockSpec((16, CELLS), lambda s: (soon(s), 0)),
            pl.BlockSpec((2 * ROWS, 2 * ROWS), lambda s: (0, 0)),
        ],
        out_specs=out_spec,
        scratch_shapes=[
            pltpu.VMEM((GROUP, GROUP, 2, 16, LANES), jnp.float32),
            pltpu.VMEM((2 * ROWS, CELLS * LANES), jnp.bfloat16),
        ],
        compiler_params=pltpu.CompilerParams(vmem_limit_bytes=VMEM_LIMIT),
        cost_estimate=pl.CostEstimate(flops=2 * 1024 * 2048 * 2048, bytes_accessed=8 << 20, transcendentals=0),
        name="u_first" if early else "u_last",
    )(place, w_value, after, *cells, tw_cos, tw_sin, jnp.asarray(short_table()))


def arrange_kernel(col_ref, *refs):
    one, (two_ref, rows_ref, cols_ref, out_ref, picks, held) = refs[:GROUP], refs[GROUP:]
    places = [lax.rem(col_ref[0] // 2 + 4 - n // 2, 4) * 2 + lax.rem(col_ref[0] + n, 2) for n in range(GROUP)]

    @pl.when(pl.program_id(0) == 0)
    def _():
        q = lax.broadcasted_iota(jnp.int32, (LANES, BLOCK), 0)
        m = lax.broadcasted_iota(jnp.int32, (LANES, BLOCK), 1)
        for n, j in enumerate(places):
            picks[n] = jnp.where(m == GROUP * q + j, 1.0, 0.0).astype(jnp.bfloat16)

    total = None
    for n, j in enumerate(places):
        other = [two_ref[0, r, j].astype(jnp.float32) + two_ref[1, r, j].astype(jnp.float32) for r in range(2)]
        cells = (one[n][...].astype(jnp.float32) + jnp.concatenate(other, axis=0)).astype(jnp.bfloat16)
        part = jnp.dot(cells, picks[n], preferred_element_type=jnp.float32)
        total = part if total is None else total + part
    total = total * (cols_ref[...] / NPIX)
    for part in range(GROUP):
        lanes = slice(part * LANES, (part + 1) * LANES)
        held[part] = total[:, lanes]
        for g in range(8):
            out_ref[g, :, lanes] = held[part, pl.ds(g, 16, 8), :] * rows_ref[g]


def arrange(col, one, two, taper_rows, taper_cols):
    tile = pl.BlockSpec((8, 16, 1), lambda s: (0, s, 0))
    return pl.pallas_call(
        arrange_kernel,
        grid=(CELLS // 16,),
        out_shape=jax.ShapeDtypeStruct((8, CELLS, BLOCK), jnp.float32),
        in_specs=[pl.BlockSpec(memory_space=pltpu.SMEM)]
        + [pl.BlockSpec((LANES, LANES), lambda s: (s, 0))] * GROUP
        + [
            pl.BlockSpec((LAYERS_AXIS, 2, GROUP, CELLS, LANES), lambda s: (0, s, 0, 0, 0)),
            tile,
            pl.BlockSpec((1, BLOCK), lambda s: (0, 0)),
        ],
        out_specs=pl.BlockSpec((8, 16, BLOCK), lambda s: (0, s, 0)),
        scratch_shapes=[
            pltpu.VMEM((GROUP, LANES, BLOCK), jnp.bfloat16),
            pltpu.VMEM((GROUP, LANES, LANES), jnp.float32),
        ],
        compiler_params=pltpu.CompilerParams(vmem_limit_bytes=VMEM_LIMIT),
        name="arrange",
    )(col, *one, two, taper_rows.reshape(8, CELLS, 1), taper_cols).reshape(8 * CELLS, BLOCK)


def columns_kernel(_, __, *refs):
    for cut, out in zip(refs[:GROUP], refs[GROUP:]):
        out[...] = cut[0]


def across_row(place, n):
    return (place // 4 + n // 4) % 2 * 4 + (place + n) % 4


def across_col(place, n):
    return (place // 2 + n // 2) % 4 * 2 + (place + n) % 2


def columns(grids, k, row, after):
    rows = 256
    cut = lambda n: pl.BlockSpec((1, rows, 2 * LANES), lambda s, place: (k, s, across_row(place[0], n)))
    return pl.pallas_call(
        columns_kernel,
        grid_spec=pltpu.PrefetchScalarGridSpec(
            num_scalar_prefetch=1,
            grid=(BLOCK // rows,),
            in_specs=[pl.BlockSpec(memory_space=pl.ANY)] + [cut(n) for n in range(GROUP)],
            out_specs=[pl.BlockSpec((rows, 2 * LANES), lambda s, place: (s, 0))] * GROUP,
        ),
        out_shape=[jax.ShapeDtypeStruct((BLOCK, 2 * LANES), grids.dtype)] * GROUP,
        compiler_params=pltpu.CompilerParams(vmem_limit_bytes=VMEM_LIMIT),
        name="columns",
    )(row, after, *[grids] * GROUP)


def around(blocks, axis, across, order):
    moved = {0: blocks[0]}
    for n in order:
        moved[n] = lax.ppermute(blocks[n], axis, [(c, across(c, n)) for c in range(GROUP)])
    return [moved[n] for n in range(GROUP)]


def gate_kernel(*refs):
    del refs


def gate(value, *others):
    return pl.pallas_call(
        gate_kernel,
        out_shape=jax.ShapeDtypeStruct(value.shape, value.dtype),
        in_specs=[pl.BlockSpec(memory_space=pl.ANY)] * (1 + len(others)),
        out_specs=pl.BlockSpec(memory_space=pl.ANY),
        input_output_aliases={0: 0},
        name="gate",
    )(value, *others)


def swap(blocks, axes):
    return lax.all_to_all(blocks, axes, split_axis=0, concat_axis=0, tiled=True)


def on_device(grids, taper, w_steps):
    lay, row, col = lax.axis_index("layer"), lax.axis_index("row"), lax.axis_index("col")
    corner_u = (BLOCK * row + col).astype(jnp.int32).reshape(1)
    corner_v = (8 * CELLS * col + 8 * row).astype(jnp.int32).reshape(1)
    taper_cols = lax.dynamic_slice_in_dim(taper, BLOCK * row, BLOCK).reshape(1, BLOCK)
    taper_rows = lax.dynamic_slice_in_dim(taper, 8 * CELLS * (GROUP * lay + col), 8 * CELLS).reshape(8 * CELLS, 1)
    tables_u = [jnp.asarray(t) for t in row_tables()]
    tables_v = [jnp.asarray(t) for t in spread_tables()]
    own_u = [lax.dynamic_index_in_dim(t, row, 0, keepdims=False) for t in tables_u]
    own_v = [lax.dynamic_index_in_dim(t, col - col % 2, 0, keepdims=False) for t in tables_v]
    first_u, first_v = [t[0] for t in tables_u], [t[0] for t in tables_v]
    w_one, w_two = w_steps[:1], w_steps[1:]
    scalar = lambda value: value.astype(jnp.int32).reshape(1)

    side, place_y = col % 2, col // 2
    cells = grids.reshape(grids.shape[0], GROUP // 2, 2, ROWS, 2 * BLOCK)
    take = lambda k: lax.dynamic_slice(cells, (0, 0, k, 0, 0), (1, GROUP // 2, 1, ROWS, 2 * BLOCK))
    mine, give = (take(k).reshape(GROUP // 2, ROWS, 2 * BLOCK) for k in (side, 1 - side))
    got = lax.ppermute(give, "col", [(c, c ^ 1) for c in range(GROUP)])
    half = {}

    def along_y(n, *earlier):
        target = (place_y + n) % (GROUP // 2)
        block = jnp.stack([lax.dynamic_index_in_dim(t, target, 0, keepdims=False) for t in (mine, got)])
        if earlier:
            block = gate(block, *earlier)
        moved = lax.ppermute(block, "col", [(c, (c + 2 * n) % GROUP) for c in range(GROUP)]) if n else block
        half[-n % (GROUP // 2)] = moved
        return block

    along_y(1)
    begun = along_y(3)
    other = around(columns(grids, 1, scalar(row), begun), "row", across_row, (1, 3, 4, 5, 7, 2, 6))
    along_y(2, half[1], half[3], other[1], other[3], other[4])
    along_y(0)
    half = [half[n] for n in range(GROUP // 2)]
    half = along_v(True, half, *own_v, scalar(side), corner_v, w_one, w_one)
    half = gate(half, *other[1:])
    other = [other[n // 4 * 4 + -n % 4].reshape(GROUP, ROWS, 2 * LANES) for n in range(GROUP)]
    other = along_u(True, other, *own_u, corner_u, scalar(row), half)
    half = swap(half.reshape(CELLS, 2, ROWS, LANES), ("row", "col"))
    other = swap(other.reshape(CELLS, 2, ROWS, LANES), ("row", "col"))

    one = along_u(False, [half], *first_u, corner_u, w_one, w_one)
    two = along_v(False, [other.reshape(GROUP, GROUP, 2, ROWS, LANES)], *first_v, scalar(side), corner_v, w_two, one)
    one = one.reshape(LAYERS_AXIS, GROUP, 8 * CELLS, LANES)
    keep = lax.dynamic_index_in_dim(one, lay, 0, keepdims=False)
    send = lax.dynamic_index_in_dim(one, 1 - lay, 0, keepdims=False)
    send = lax.ppermute(send, "layer", [(0, 1), (1, 0)])
    two = gate(two.reshape(LAYERS_AXIS * GROUP, GROUP, CELLS, LANES), send)
    one = (keep.astype(jnp.float32) + send.astype(jnp.float32)).astype(jnp.bfloat16)
    two = swap(two, ("layer", "row")).reshape(LAYERS_AXIS, GROUP, GROUP, CELLS, LANES)
    one = [lax.dynamic_index_in_dim(one, across_col(col, n), 0, keepdims=False) for n in range(GROUP)]
    one = around(one, "col", across_col, (2, 3, 6, 7, 4, 5, 1))
    return arrange(scalar(col), one, two, taper_rows, taper_cols)


def solution(mesh):
    placed = (P("layer", "row", "col"), P(), P("layer"))
    return jax.shard_map(
        on_device, mesh=mesh, in_specs=placed, out_specs=P(("layer", "col"), "row"), check_vma=False
    )
```
